512 devices in a mesh: tensor: 32 (over z, y_hi, core), replay: 16 (over x, y_lo).
Axes of the slice: x: 4, y: 8 (y_hi: 2, y_lo: 4; y = y_hi * 4 + y_lo), z: 8, core: 2. Of those that a mesh axis runs over, the one named last changes fastest.
Arguments:
- x_store: bfloat16 [2048, 4096], P('replay', 'tensor'), may hold values from -6 to 6
- attn_store: bfloat16 [2048, 4096], P('replay', 'tensor'), may hold values from -6 to 6
- replay_idx: int32 [16, 128], P('replay'), may hold values from 0 to 127
- w_qkv: bfloat16 [6144, 4096], P('tensor', 'replay'), may hold values from -0.09375 to 0.09375
- w_out: bfloat16 [4096, 4096], P('tensor', 'replay'), may hold values from -0.09375 to 0.09375
- d_qkv: bfloat16 [2048, 6144], P('replay', 'tensor'), may hold values from -6 to 6
- d_out: bfloat16 [2048, 4096], P('replay', 'tensor'), may hold values from -6 to 6
Outputs:
- qkv: float32 [2048, 6144], P('replay', 'tensor')
- out: float32 [2048, 4096], P('replay', 'tensor')
- grad_inputs: float32 [2048, 4096], P('replay', 'tensor')
- grad_attn: float32 [2048, 4096], P('replay', 'tensor')
- grad_wqkv: bfloat16 [6144, 4096], P('tensor')
- grad_wout: bfloat16 [4096, 4096], P('tensor')
The draws below stay inside these ranges and needn't reach their ends.
Inputs may be any that keep to these rules, and one draw needn't show every extreme that they name: `replay_idx`: rows are sampled with replacement within each group's store of 128 rows.
All inputs are finite; a program needn't handle non-finite values.
Results may differ from the reference program's by a relative error of at most 0.023.
Values may be sent and summed in bfloat16 or wider, within the bound.
A program may use at most 64 MiB of HBM per device.

```python
import jax
import jax.numpy as jnp
from jax import lax

DW = 4096
QW = 4096
ROWS = 128
QKVW = 6144
GROUPS = 16
TOKENS = 2048


def touch_ends(array, key, least, high):
    longest = array.shape.index(max(array.shape))
    spots = []
    for shift in (0, 1):
        where = [jax.random.randint(jax.random.fold_in(key, axis), (), 0, length) for axis, length in enumerate(array.shape)]
        where[longest] = (where[longest] + shift) % array.shape[longest]
        spots.append(tuple(where))
    return array.at[spots[0]].set(least).at[spots[1]].set(high)


def block_levels(stream_key, dims, cuts, least, top_value):
    gain, own = 1.0, jax.random.fold_in(stream_key, 6)
    for axis_at, blocks in cuts:
        draws = jnp.exp(jax.random.uniform(jax.random.fold_in(own, axis_at), (blocks,), jnp.float32, least / len(cuts), top_value / len(cuts)))
        gain = gain * jnp.repeat(draws, dims[axis_at] // blocks).reshape([-1 if axis == axis_at else 1 for axis in range(len(dims))])
    return gain


def noise(rng, extent, deviation, limit, pieces=(), kind=jnp.bfloat16):
    loudness = block_levels(rng, extent, pieces, -0.22, 0.18) if pieces else 1.0
    values = jax.random.normal(rng, extent, jnp.float32) * deviation * loudness
    return jnp.minimum(jnp.maximum(values, -limit), limit).astype(kind)


def setup_inputs(seed: int = 0) -> dict:
    keys = jax.random.split(jax.random.key(seed), 8)
    return {
        "x_store": noise(keys[0], (TOKENS, DW), 1.0, 6.0, ((0, 16), (1, 32))),
        "attn_store": noise(keys[1], (TOKENS, QW), 1.0, 6.0, ((0, 16), (1, 32))),
        "replay_idx": touch_ends(jax.random.randint(keys[2], (GROUPS, ROWS), 0, ROWS), jax.random.fold_in(keys[2], 1), 0, ROWS - 1).astype(jnp.int32),
        "w_qkv": noise(keys[3], (QKVW, DW), DW ** -0.5, 0.09375, ((0, 32), (1, 16))),
        "w_out": noise(keys[4], (QW, DW), QW ** -0.5, 0.09375, ((0, 32), (1, 16))),
        "d_qkv": noise(keys[5], (TOKENS, QKVW), 1.0, 6.0, ((0, 16), (1, 32))),
        "d_out": noise(keys[6], (TOKENS, DW), 1.0, 6.0, ((0, 16), (1, 32))),
    }


def to_half(value):
    return lax.optimization_barrier(value.astype(jnp.bfloat16)).astype(jnp.float32)


def reference(x_store, attn_store, replay_idx, w_qkv, w_out, d_qkv, d_out):
    offsets = (jnp.arange(GROUPS, dtype=jnp.int32) * ROWS)[:, None]
    picked = (replay_idx + offsets).reshape(-1).astype(jnp.int32)
    inputs = jnp.take(x_store, picked, axis=0)
    heads = jnp.take(attn_store, picked, axis=0)
    qkv = lax.dot_general(inputs, w_qkv, (((1,), (1,)), ((), ())), preferred_element_type=jnp.float32)
    out_total = jnp.dot(heads, w_out, preferred_element_type=jnp.float32)
    input_total = jnp.dot(d_qkv, w_qkv, preferred_element_type=jnp.float32)
    grad_attn = lax.dot_general(d_out, w_out, (((1,), (1,)), ((), ())), preferred_element_type=jnp.float32)

    def grad_term(carry, index):
        total_qkv, total_out = carry
        start = (index * ROWS).astype(jnp.int32)
        x_rows = lax.dynamic_slice_in_dim(inputs, start, ROWS, 0)
        h_rows = lax.dynamic_slice_in_dim(heads, start, ROWS, 0)
        dq_rows = lax.dynamic_slice_in_dim(d_qkv, start, ROWS, 0)
        do_rows = lax.dynamic_slice_in_dim(d_out, start, ROWS, 0)
        term_qkv = lax.dot_general(dq_rows, x_rows, (((0,), (0,)), ((), ())), preferred_element_type=jnp.float32) / ROWS
        term_out = lax.dot_general(h_rows, do_rows, (((0,), (0,)), ((), ())), preferred_element_type=jnp.float32) / ROWS
        return (total_qkv + to_half(term_qkv), total_out + to_half(term_out)), None

    start_carry = (jnp.zeros((QKVW, DW), jnp.float32), jnp.zeros((QW, DW), jnp.float32))
    grads, _ = lax.scan(grad_term, start_carry, jnp.arange(GROUPS, dtype=jnp.int32))
    return (qkv, out_total, input_total, grad_attn,
            grads[0].astype(jnp.bfloat16), grads[1].astype(jnp.bfloat16))
```

```python
import jax
import jax.numpy as jnp
from jax import lax
from jax.experimental import pallas as pl
from jax.experimental.pallas import tpu as pltpu
from jax.sharding import PartitionSpec as P

BF, F32 = jnp.bfloat16, jnp.float32
MESH = pl.DeviceIdType.MESH
ROWS, QF, OF, QO = 128, 192, 128, 320
PARTS = ((0, QF), (QF, OF))


def dot(a, b, ca, cb):
    return lax.dot_general(a, b, (((ca,), (cb,)), ((), ())), preferred_element_type=F32)


def make_labels():
    table = {}

    def label(*key):
        return table.setdefault(key, len(table))

    return table, label


TABLE, LABEL = make_labels()


def kernel(x_ref, a_ref, idx_ref, wq_ref, wo_ref, dq_ref, do_ref,
           qkv_ref, out_ref, gin_ref, gat_ref, gwq_ref, gwo_ref,
           own, dh, wall, xb, gsend, gkeep, gacc, gr1, gr2, gout,
           ysend, yrecv, ykeep, esend, erecv, part, zsend, zrecv, scsend, screcv,
           ssem, rsem):
    t, r = lax.axis_index("tensor"), lax.axis_index("replay")
    c, yh, z = lax.rem(t, 2), lax.rem(t // 2, 2), t // 4
    x, yl = r // 4, lax.rem(r, 4)
    h = lax.rem(z, 2)

    def device(x_, yl_, yh_, z_, c_):
        return ((z_ * 2 + yh_) * 2 + c_, x_ * 4 + yl_)

    def xat(k):
        return lax.rem(x + k + 4, 4)

    def yat(k):
        return lax.rem(yl + k + 4, 4)

    def zat(k):
        return lax.rem(z + k + 8, 8)

    xdev = {k: device(xat(k), yl, yh, z, c) for k in (1, -1)}
    zdev = {k: device(x, yl, yh, zat(k), c) for k in (1, -1)}
    ydev = {k: device(x, yat(k), yh, z, c) for k in (1, 2, 3)}
    sib = device(x, yl, yh, z, 1 - c)
    q = 2 * h + yh
    zt = 2 * (z // 2) + yl // 2
    alone = yl == q
    yhs = (yh, 1 - yh)
    to_dev = [device(x, q, v, zt, c) for v in yhs]
    from_dev = [device(x, 2 * h + v, lax.rem(yl, 2), zt, c) for v in yhs]

    bar = pltpu.get_barrier_semaphore()
    peers = list(xdev.values()) + list(zdev.values()) + list(ydev.values()) + [sib]
    for d in peers + to_dev + from_dev:
        pl.semaphore_signal(bar, inc=1, device_id=d, device_id_type=MESH)

    sent = []

    def desc(src, dst, s, rs, dev):
        return pltpu.make_async_remote_copy(
            src_ref=src, dst_ref=dst, send_sem=ssem.at[s], recv_sem=rsem.at[rs],
            device_id=dev, device_id_type=MESH)

    def send(src, dst, dev, *key):
        s = LABEL(*key)
        cp = desc(src, dst, s, s, dev)
        cp.start()
        sent.append(cp)

    def arrive(dst, *key):
        s = LABEL(*key)
        desc(dst, dst, s, s, sib).wait_recv()

    iota0 = lax.broadcasted_iota(jnp.int32, (ROWS, ROWS), 0)
    iota1 = lax.broadcasted_iota(jnp.int32, (ROWS, ROWS), 1)
    pick = jnp.where(iota0 == idx_ref[...], 1.0, 0.0).astype(BF)
    eye = jnp.where(iota0 == iota1, 1.0, 0.0).astype(BF)
    own[0] = dot(pick, x_ref[...], 0, 0).astype(BF)
    own[1] = do_ref[...]
    dh[yl, 0:QF] = dot(dq_ref[...], eye, 0, 0).astype(BF)
    dh[yl, QF:QO] = dot(a_ref[...], pick, 0, 0).astype(BF)
    wall[x, 0:QF] = wq_ref[...]
    wall[x, QF:QO] = wo_ref[...]
    pl.semaphore_wait(bar, len(peers) + 4)

    def turn(arr):
        dst = xb.at[arr, c, zt, pl.ds(pl.multiple_of(lax.rem(yl, 2) * ROWS, ROWS), ROWS)]
        rs = LABEL("turn", arr, 0) + lax.rem(yl, 2)
        assert LABEL("turn", arr, 1) == LABEL("turn", arr, 0) + 1

        @pl.when(alone)
        def _():
            pltpu.make_async_copy(own.at[arr], dst, rsem.at[rs]).start()

        @pl.when(jnp.logical_not(alone))
        def _():
            desc(own.at[arr], dst, LABEL("turn", arr, 0), rs, to_dev[0]).start()

        desc(own.at[arr], dst, LABEL("turn", arr, 1), rs, to_dev[1]).start()

    def turn_sent(arr):
        @pl.when(jnp.logical_not(alone))
        def _():
            desc(own.at[arr], own.at[arr], LABEL("turn", arr, 0), 0, to_dev[0]).wait_send()

        desc(own.at[arr], own.at[arr], LABEL("turn", arr, 1), 0, to_dev[1]).wait_send()

    turn(0)
    for k in (1, 2, 3):
        send(dh.at[yl], dh.at[yl], ydev[k], "dh", k)
    turn(1)
    for k in (1, -1):
        send(wall.at[x], wall.at[x], xdev[k], "w", k)

    def zvalid(step, arr, way):
        return step < 4 or (arr == 0) == (way == 1)

    def zpass(step, arr):
        for way in (1, -1):
            if zvalid(step, arr, way):
                at = zat(-way * (step - 1))
                send(xb.at[arr, c, at], xb.at[arr, c, at], zdev[way], "z", step, arr, way)

    def ztake(step, arr):
        for way in (1, -1):
            if zvalid(step, arr, way):
                at = zat(-way * step)
                arrive(xb.at[arr, c, at], "z", step, arr, way)

    def zgive(step, arr):
        for way in (1, -1):
            if zvalid(step, arr, way):
                at = zat(-way * step)
                send(xb.at[arr, c, at], xb.at[arr, c, at], sib, "s", step, arr, way)

    for arr in (0, 1):
        for v in (0, 1):
            arrive(xb.at[arr, c, z, pl.ds(v * ROWS, ROWS)], "turn", arr, v)
        zpass(1, arr)
        send(xb.at[arr, c, z], xb.at[arr, c, z], sib, "s", 0, arr)

    A, B = (0, QO // 2), (QO // 2, QO // 2)
    for k, half in ((1, A), (-1, B)):
        arrive(wall.at[xat(-k)], "w", k)
        piece = wall.at[xat(-k), pl.ds(*half)]
        send(piece, piece, xdev[k], "w2", k)

    for step in (1, 2, 3):
        for arr in (0, 1):
            ztake(step, arr)
            zpass(step + 1, arr)
            zgive(step, arr)
    for arr in (0, 1):
        ztake(4, arr)
        zgive(4, arr)

    for k in (1, 2, 3):
        arrive(dh.at[yat(-k)], "dh", k)

    def other(arr):
        arrive(xb.at[arr, 1 - c, z], "s", 0, arr)
        for step in (1, 2, 3, 4):
            for way in (1, -1):
                if zvalid(step, arr, way):
                    arrive(xb.at[arr, 1 - c, zat(-way * step)], "s", step, arr, way)

    def block(arr, xp):
        return jnp.concatenate(
            [jnp.concatenate([xb[arr, 0, 2 * xp + v], xb[arr, 1, 2 * xp + v]], axis=1) for v in (0, 1)], axis=0)

    def grads(p):
        lo, n = PARTS[p]
        half = n // 2
        lhs = jnp.concatenate([dh[g, lo:lo + n] for g in range(4)], axis=1)

        def term(k):
            return dot(lhs, block(p, xat(k)), 1, 0) * (1.0 / ROWS)

        gsend[lo:lo + n] = term(2).astype(BF)
        for k, at in ((1, lo), (-1, lo + half)):
            send(gsend.at[pl.ds(at, half)], gr1.at[pl.ds(at, half)], xdev[k], "g1", p, k)
        for i, k in enumerate((1, -1, 0)):
            gkeep[i, lo:lo + n] = term(k)

    def grads2(p):
        lo, n = PARTS[p]
        half = n // 2
        for i, (k, at) in enumerate(((1, lo), (-1, lo + half))):
            arrive(gr1.at[pl.ds(at, half)], "g1", p, k)
            rest = lo + half if k == 1 else lo
            gacc[i, at:at + half] = (gkeep[i, at:at + half] + gr1[at:at + half].astype(F32)).astype(BF)
            gacc[i, rest:rest + half] = gkeep[i, rest:rest + half].astype(BF)
            send(gacc.at[i, pl.ds(lo, n)], gr2.at[i, pl.ds(lo, n)], xdev[k], "g2", p, k)

    def grads3(p):
        lo, n = PARTS[p]
        for i, k in enumerate((1, -1)):
            arrive(gr2.at[i, pl.ds(lo, n)], "g2", p, k)
        gout[r, lo:lo + n] = (gkeep[2, lo:lo + n] + gr2[0, lo:lo + n].astype(F32)
                              + gr2[1, lo:lo + n].astype(F32)).astype(BF)
        piece = gout.at[r, pl.ds(lo, n)]
        for k in (1, -1):
            send(piece, piece, xdev[k], "ax", p, 0, k)
        for k in (1, 2, 3):
            send(piece, piece, ydev[k], "ay", p, k)

    def gather_y(p, j):
        lo, n = PARTS[p]
        piece = gout.at[x * 4 + yat(-j), pl.ds(lo, n)]
        arrive(piece, "ay", p, j)
        for k in (1, -1):
            send(piece, piece, xdev[k], "ax", p, j, k)

    def gather_x(p, j):
        lo, n = PARTS[p]
        half = n // 2
        for k, at in ((1, lo), (-1, lo + half)):
            row = xat(-k) * 4 + yat(-j)
            arrive(gout.at[row, pl.ds(lo, n)], "ax", p, j, k)
            piece = gout.at[row, pl.ds(at, half)]
            send(piece, piece, xdev[k], "ar", p, j, k)

    def gather_end(p, j):
        lo, n = PARTS[p]
        half = n // 2
        for k, at in ((1, lo), (-1, lo + half)):
            arrive(gout.at[xat(2) * 4 + yat(-j), pl.ds(at, half)], "ar", p, j, k)

    other(0)
    grads(0)
    other(1)
    grads(1)

    for k, half in ((1, A), (-1, B)):
        arrive(wall.at[xat(2), pl.ds(*half)], "w2", k)
    for arr, (lo, n) in enumerate(PARTS):
        w = jnp.concatenate([wall[v, lo:lo + n] for v in range(4)], axis=1)
        for g in range(4):
            y = dot(dh[g, lo:lo + n], w, 0, 0)
            rows = slice(g % 2 * ROWS, g % 2 * ROWS + ROWS)
            for xp in range(4):
                left, right = y[:, xp * 256:xp * 256 + 128], y[:, xp * 256 + 128:xp * 256 + 256]
                part[arr, 2 * xp + g // 2, rows] = jnp.where(c == 0, left, right)
                esend[arr, 2 * xp + g // 2, rows] = jnp.where(c == 0, right, left).astype(BF)
        send(esend.at[arr], erecv.at[arr], sib, "e", arr)

    grads2(0)
    grads2(1)

    for arr, (lo, n) in enumerate(PARTS):
        w = jnp.concatenate([wall[v, lo:lo + n] for v in range(4)], axis=1)
        for v in (0, 1):
            rhs = jnp.concatenate([xb[arr, cc, 2 * xp + v] for xp in range(4) for cc in (0, 1)], axis=1)
            y = dot(w, rhs, 1, 1)
            for j in (0, 1):
                ykeep[2 * v + j, lo:lo + n] = y[:, j * ROWS:(j + 1) * ROWS]
                ysend[2 * v + j, lo:lo + n] = y[:, j * ROWS:(j + 1) * ROWS].astype(BF)
    for k in (1, 2, 3):
        send(ysend.at[yat(k)], yrecv.at[k - 1], ydev[k], "y", k)

    def zadd(step):
        for arr in (0, 1):
            if step == 1:
                arrive(erecv.at[arr], "e", arr)
                for v in range(8):
                    part[arr, v] = part[arr, v] + erecv[arr, v].astype(F32)
            for way in (1, -1):
                i = (1 - way) // 2
                if step == 1 and (arr == 0) != (way == 1):
                    continue
                at = zat(way * (5 - step))
                value = part[arr, at]
                if step > 2 or (step == 2 and (arr == 0) == (way == 1)):
                    arrive(zrecv.at[arr, i, step - 2], "r", step - 1, arr, way)
                    value = value + zrecv[arr, i, step - 2].astype(F32)
                zsend[arr, i, step - 1] = value.astype(BF)
                send(zsend.at[arr, i, step - 1], zrecv.at[arr, i, step - 1], zdev[way], "r", step, arr, way)

    def zend():
        for arr in (0, 1):
            value = part[arr, z]
            for way in (1, -1):
                i = (1 - way) // 2
                arrive(zrecv.at[arr, i, 3], "r", 4, arr, way)
                value = value + zrecv[arr, i, 3].astype(F32)
            value = value.astype(BF)
            for j in (0, 1):
                scsend[j, arr] = value[j * ROWS:(j + 1) * ROWS]

    def scatter():
        rs = LABEL("sc", 0) + yh
        assert LABEL("sc", 1) == LABEL("sc", 0) + 1
        dst = screcv.at[yh]

        @pl.when(alone)
        def _():
            pltpu.make_async_copy(scsend.at[yhs[0]], dst, rsem.at[rs]).start()

        @pl.when(jnp.logical_not(alone))
        def _():
            desc(scsend.at[yhs[0]], dst, LABEL("sc", 0), rs, from_dev[0]).start()

        desc(scsend.at[yhs[1]], dst, LABEL("sc", 1), rs, from_dev[1]).start()

    def scatter_end():
        for v in (0, 1):
            arrive(screcv.at[v], "sc", v)
        gin_ref[...] = screcv[0, 0].astype(F32) + screcv[1, 0].astype(F32)
        out_ref[...] = screcv[0, 1].astype(F32) + screcv[1, 1].astype(F32)

        @pl.when(jnp.logical_not(alone))
        def _():
            desc(scsend.at[0], scsend.at[0], LABEL("sc", 0), 0, from_dev[0]).wait_send()

        desc(scsend.at[0], scsend.at[0], LABEL("sc", 1), 0, from_dev[1]).wait_send()

    zadd(1)
    grads3(0)
    grads3(1)
    zadd(2)
    for p in (0, 1):
        gather_y(p, 1)
    for p in (0, 1):
        gather_x(p, 0)
    zadd(3)
    for p in (0, 1):
        gather_y(p, 2)
        gather_y(p, 3)
    zadd(4)
    for p in (0, 1):
        gather_x(p, 1)
    zend()
    scatter()
    for p in (0, 1):
        gather_x(p, 2)

    total = ykeep[yl]
    for k in (1, 2, 3):
        arrive(yrecv.at[k - 1], "y", k)
        total = total + yrecv[k - 1].astype(F32)
    qkv_ref[...] = total[0:QF].T
    gat_ref[...] = total[QF:QO].T

    for p in (0, 1):
        gather_x(p, 3)
    scatter_end()
    for p in (0, 1):
        for j in range(4):
            gather_end(p, j)
    for row in range(16):
        gwq_ref[:, row * 256:(row + 1) * 256] = gout[row, 0:QF]
        gwo_ref[:, row * 256:(row + 1) * 256] = gout[row, QF:QO]
    turn_sent(0)
    turn_sent(1)
    for cp in sent:
        cp.wait_send()


def shards(*args):
    vm = pl.BlockSpec(memory_space=pltpu.VMEM)
    shapes = [((ROWS, QF), F32), ((ROWS, OF), F32), ((ROWS, 128), F32), ((ROWS, 128), F32),
              ((QF, 4096), BF), ((OF, 4096), BF)]
    scratch = [
        ((2, ROWS, 128), BF),
        ((4, QO, ROWS), BF),
        ((4, QO, 256), BF),
        ((2, 2, 8, 256, 128), BF),
        ((QO, 256), BF),
        ((3, QO, 256), F32),
        ((2, QO, 256), BF),
        ((QO, 256), BF),
        ((2, QO, 256), BF),
        ((16, QO, 256), BF),
        ((4, QO, ROWS), BF),
        ((3, QO, ROWS), BF),
        ((4, QO, ROWS), F32),
        ((2, 8, 256, 128), BF),
        ((2, 8, 256, 128), BF),
        ((2, 8, 256, 128), F32),
        ((2, 2, 4, 256, 128), BF),
        ((2, 2, 4, 256, 128), BF),
        ((2, 2, ROWS, 128), BF),
        ((2, 2, ROWS, 128), BF),
    ]
    count = 160
    return tuple(pl.pallas_call(
        kernel,
        name="critic_layer",
        out_shape=[jax.ShapeDtypeStruct(s, d) for s, d in shapes],
        in_specs=[vm] * 7,
        out_specs=[vm] * 6,
        scratch_shapes=[pltpu.VMEM(s, d) for s, d in scratch]
        + [pltpu.SemaphoreType.DMA((count,)), pltpu.SemaphoreType.DMA((count,))],
        compiler_params=pltpu.CompilerParams(
            collective_id=0, has_side_effects=True, vmem_limit_bytes=40 << 20),
    )(*args))


def solution(mesh):
    in_specs = (
        P("replay", "tensor"),
        P("replay", "tensor"),
        P("replay", None),
        P("tensor", "replay"),
        P("tensor", "replay"),
        P("replay", "tensor"),
        P("replay", "tensor"),
    )
    out_specs = (
        P("replay", "tensor"),
        P("replay", "tensor"),
        P("replay", "tensor"),
        P("replay", "tensor"),
        P("tensor", None),
        P("tensor", None),
    )
    return jax.shard_map(shards, mesh=mesh, in_specs=in_specs, out_specs=out_specs, check_vma=False)
```

```python
import jax
import jax.numpy as jnp
from jax import lax
from jax.experimental import pallas as pl
from jax.experimental.pallas import tpu as pltpu
from jax.sharding import PartitionSpec as P

BF, F32 = jnp.bfloat16, jnp.float32
MESH = pl.DeviceIdType.MESH
ROWS, QF, OF, QO = 128, 192, 128, 320
PARTS = ((0, QF), (QF, OF))


def dot(a, b, ca, cb):
    return lax.dot_general(a, b, (((ca,), (cb,)), ((), ())), preferred_element_type=F32)


def make_labels():
    table = {}

    def label(*key):
        return table.setdefault(key, len(table))

    return table, label


TABLE, LABEL = make_labels()


def kernel(x_ref, a_ref, idx_ref, wq_ref, wo_ref, dq_ref, do_ref,
           qkv_ref, out_ref, gin_ref, gat_ref, gwq_ref, gwo_ref,
           xin, ain, idx, own, dh, wall, xb, gsend, gkeep, gr, gout,
           ysend, yrecv, ykeep, esend, erecv, part, zsend, zrecv, scsend, screcv,
           ssem, rsem, lsem):
    t, r = lax.axis_index("tensor"), lax.axis_index("replay")
    c, yh, z = lax.rem(t, 2), lax.rem(t // 2, 2), t // 4
    x, yl = r // 4, lax.rem(r, 4)
    h = lax.rem(z, 2)

    def device(x_, yl_, yh_, z_, c_):
        return ((z_ * 2 + yh_) * 2 + c_, x_ * 4 + yl_)

    def xat(k):
        return lax.rem(x + k + 4, 4)

    def yat(k):
        return lax.rem(yl + k + 4, 4)

    def zat(k):
        return lax.rem(z + k + 8, 8)

    xdev = {k: device(xat(k), yl, yh, z, c) for k in (1, -1, 2)}
    zdev = {k: device(x, yl, yh, zat(k), c) for k in (1, -1)}
    ydev = {k: device(x, yat(k), yh, z, c) for k in (1, 2, 3)}
    sib = device(x, yl, yh, z, 1 - c)
    q = 2 * h + yh
    zt = 2 * (z // 2) + yl // 2
    alone = yl == q
    yhs = (yh, 1 - yh)
    to_dev = [device(x, q, v, zt, c) for v in yhs]
    from_dev = [device(x, 2 * h + v, lax.rem(yl, 2), zt, c) for v in yhs]

    loads = [
        pltpu.make_async_copy(src, dst, lsem.at[i])
        for i, (src, dst) in enumerate((
            (idx_ref, idx), (x_ref, xin), (do_ref, own.at[1]),
            (wq_ref, wall.at[x, pl.ds(0, QF)]), (wo_ref, wall.at[x, pl.ds(QF, OF)]),
            (dq_ref, dh.at[yl, pl.ds(0, QF)]), (a_ref, ain)))
    ]
    for cp in loads:
        cp.start()

    bar = pltpu.get_barrier_semaphore()
    peers = list(xdev.values()) + list(zdev.values()) + list(ydev.values()) + [sib]
    for d in peers + to_dev + from_dev:
        pl.semaphore_signal(bar, inc=1, device_id=d, device_id_type=MESH)

    sent = []

    def desc(src, dst, s, rs, dev):
        return pltpu.make_async_remote_copy(
            src_ref=src, dst_ref=dst, send_sem=ssem.at[s], recv_sem=rsem.at[rs],
            device_id=dev, device_id_type=MESH)

    def send(src, dst, dev, *key):
        s = LABEL(*key)
        cp = desc(src, dst, s, s, dev)
        cp.start()
        sent.append(cp)

    def arrive(dst, *key):
        s = LABEL(*key)
        desc(dst, dst, s, s, sib).wait_recv()

    iota0 = lax.broadcasted_iota(jnp.int32, (ROWS, ROWS), 0)
    loads[0].wait()
    loads[1].wait()
    pick = jnp.where(iota0 == idx[...], 1.0, 0.0).astype(BF)
    own[0] = dot(pick, xin[...], 0, 0).astype(BF)
    for cp in loads[2:]:
        cp.wait()
    dh[yl, QF:QO] = dot(ain[...], pick, 0, 0).astype(BF)
    pl.semaphore_wait(bar, len(peers) + 4)

    def turn(arr):
        dst = xb.at[arr, c, zt, pl.ds(pl.multiple_of(lax.rem(yl, 2) * ROWS, ROWS), ROWS)]
        rs = LABEL("turn", arr, 0) + lax.rem(yl, 2)
        assert LABEL("turn", arr, 1) == LABEL("turn", arr, 0) + 1

        @pl.when(alone)
        def _():
            pltpu.make_async_copy(own.at[arr], dst, rsem.at[rs]).start()

        @pl.when(jnp.logical_not(alone))
        def _():
            desc(own.at[arr], dst, LABEL("turn", arr, 0), rs, to_dev[0]).start()

        desc(own.at[arr], dst, LABEL("turn", arr, 1), rs, to_dev[1]).start()

    def turn_sent(arr):
        @pl.when(jnp.logical_not(alone))
        def _():
            desc(own.at[arr], own.at[arr], LABEL("turn", arr, 0), 0, to_dev[0]).wait_send()

        desc(own.at[arr], own.at[arr], LABEL("turn", arr, 1), 0, to_dev[1]).wait_send()

    turn(0)
    turn(1)
    for k in (1, -1, 2):
        send(wall.at[x], wall.at[x], xdev[k], "w", k)

    def zways(step, arr):
        return [w for w in (1, -1) if step < 4 or (arr == 0) == (w == 1)]

    def zblock(core, step, arr, way, v):
        return xb.at[arr, core, zat(-way * step), pl.ds(v * ROWS, ROWS)]

    def zpass(step, arr, way, v):
        if way in zways(step, arr):
            piece = zblock(c, step - 1, arr, way, v)
            send(piece, piece, zdev[way], "z", step, arr, way, v)

    def zgive(step, arr, way, v):
        piece = zblock(c, step, arr, way, v)
        send(piece, piece, sib, "s", step, arr, way, v)

    def zfirst(arr):
        for v in (0, 1):
            arrive(zblock(c, 0, arr, 1, v), "turn", arr, v)
            for way in (1, -1):
                zpass(1, arr, way, v)
        for v in (0, 1):
            zgive(0, arr, 1, v)

    def zstep(step, arr):
        for v in (0, 1):
            for way in zways(step, arr):
                arrive(zblock(c, step, arr, way, v), "z", step, arr, way, v)
                if step < 4:
                    zpass(step + 1, arr, way, v)
        for v in (0, 1):
            for way in zways(step, arr):
                zgive(step, arr, way, v)

    zfirst(0)
    for k in (1, 2, 3):
        send(dh.at[yl], dh.at[yl], ydev[k], "dh", k)
    zfirst(1)
    for arr in (0, 1):
        zstep(1, arr)

    def other(arr):
        for v in (0, 1):
            arrive(zblock(1 - c, 0, arr, 1, v), "s", 0, arr, 1, v)
        for step in (1, 2, 3, 4):
            for v in (0, 1):
                for way in zways(step, arr):
                    arrive(zblock(1 - c, step, arr, way, v), "s", step, arr, way, v)

    def block(arr, xp):
        return jnp.concatenate(
            [jnp.concatenate([xb[arr, 0, 2 * xp + v], xb[arr, 1, 2 * xp + v]], axis=1) for v in (0, 1)], axis=0)

    def grads(p):
        lo, n = PARTS[p]
        lhs = jnp.concatenate([dh[g, lo:lo + n] for g in range(4)], axis=1)

        def term(k):
            return dot(lhs, block(p, xat(k)), 1, 0) * (1.0 / ROWS)

        for i, k in enumerate((2, 1, -1)):
            gsend[i, lo:lo + n] = term(k).astype(BF)
            send(gsend.at[i, pl.ds(lo, n)], gr.at[i, pl.ds(lo, n)], xdev[k], "g", p, k)
        gkeep[lo:lo + n] = term(0)

    def grads2(p):
        lo, n = PARTS[p]
        total = gkeep[lo:lo + n]
        for i, k in enumerate((2, 1, -1)):
            arrive(gr.at[i, pl.ds(lo, n)], "g", p, k)
            total = total + gr[i, lo:lo + n].astype(F32)
        gout[r, lo:lo + n] = total.astype(BF)
        piece = gout.at[r, pl.ds(lo, n)]
        for k in (1, -1):
            send(piece, piece, xdev[k], "ax", p, 0, k)
        for k in (1, 2, 3):
            send(piece, piece, ydev[k], "ay", p, k)

    def gather_y(p, j):
        lo, n = PARTS[p]
        piece = gout.at[x * 4 + yat(-j), pl.ds(lo, n)]
        arrive(piece, "ay", p, j)
        for k in (1, -1):
            send(piece, piece, xdev[k], "ax", p, j, k)

    def gather_x(p, j):
        lo, n = PARTS[p]
        half = n // 2
        for k, at in ((1, lo), (-1, lo + half)):
            row = xat(-k) * 4 + yat(-j)
            arrive(gout.at[row, pl.ds(lo, n)], "ax", p, j, k)
            piece = gout.at[row, pl.ds(at, half)]
            send(piece, piece, xdev[k], "ar", p, j, k)

    def gather_end(p, j):
        lo, n = PARTS[p]
        half = n // 2
        for k, at in ((1, lo), (-1, lo + half)):
            arrive(gout.at[xat(2) * 4 + yat(-j), pl.ds(at, half)], "ar", p, j, k)

    def eterm(arr):
        lo, n = PARTS[arr]
        w = jnp.concatenate([wall[v, lo:lo + n] for v in range(4)], axis=1)
        for g in range(4):
            y = dot(dh[g, lo:lo + n], w, 0, 0)
            rows = slice(g % 2 * ROWS, g % 2 * ROWS + ROWS)
            for xp in range(4):
                left, right = y[:, xp * 256:xp * 256 + 128], y[:, xp * 256 + 128:xp * 256 + 256]
                part[arr, 2 * xp + g // 2, rows] = jnp.where(c == 0, left, right)
                esend[arr, 2 * xp + g // 2, rows] = jnp.where(c == 0, right, left).astype(BF)
        send(esend.at[arr], erecv.at[arr], sib, "e", arr)

    def yterm(arr):
        lo, n = PARTS[arr]
        w = jnp.concatenate([wall[v, lo:lo + n] for v in range(4)], axis=1)
        for v in (0, 1):
            rhs = jnp.concatenate([xb[arr, cc, 2 * xp + v] for xp in range(4) for cc in (0, 1)], axis=1)
            y = dot(w, rhs, 1, 1)
            for j in (0, 1):
                ykeep[2 * v + j, lo:lo + n] = y[:, j * ROWS:(j + 1) * ROWS]
                ysend[2 * v + j, lo:lo + n] = y[:, j * ROWS:(j + 1) * ROWS].astype(BF)
        for k in (1, 2, 3):
            send(ysend.at[yat(k), pl.ds(lo, n)], yrecv.at[k - 1, pl.ds(lo, n)], ydev[k], "y", arr, k)

    def zadd(step):
        for arr in (0, 1):
            if step == 1:
                arrive(erecv.at[arr], "e", arr)
                for v in range(8):
                    part[arr, v] = part[arr, v] + erecv[arr, v].astype(F32)
            for way in (1, -1):
                i = (1 - way) // 2
                if step == 1 and (arr == 0) != (way == 1):
                    continue
                at = zat(way * (5 - step))
                value = part[arr, at]
                if step > 2 or (step == 2 and (arr == 0) == (way == 1)):
                    arrive(zrecv.at[arr, i, step - 2], "r", step - 1, arr, way)
                    value = value + zrecv[arr, i, step - 2].astype(F32)
                zsend[arr, i, step - 1] = value.astype(BF)
                send(zsend.at[arr, i, step - 1], zrecv.at[arr, i, step - 1], zdev[way], "r", step, arr, way)

    def zend():
        for arr in (0, 1):
            value = part[arr, z]
            for way in (1, -1):
                i = (1 - way) // 2
                arrive(zrecv.at[arr, i, 3], "r", 4, arr, way)
                value = value + zrecv[arr, i, 3].astype(F32)
            value = value.astype(BF)
            for j in (0, 1):
                scsend[j, arr] = value[j * ROWS:(j + 1) * ROWS]

    def scatter():
        rs = LABEL("sc", 0) + yh
        assert LABEL("sc", 1) == LABEL("sc", 0) + 1
        dst = screcv.at[yh]

        @pl.when(alone)
        def _():
            pltpu.make_async_copy(scsend.at[yhs[0]], dst, rsem.at[rs]).start()

        @pl.when(jnp.logical_not(alone))
        def _():
            desc(scsend.at[yhs[0]], dst, LABEL("sc", 0), rs, from_dev[0]).start()

        desc(scsend.at[yhs[1]], dst, LABEL("sc", 1), rs, from_dev[1]).start()

    def scatter_end():
        for v in (0, 1):
            arrive(screcv.at[v], "sc", v)
        gin_ref[...] = screcv[0, 0].astype(F32) + screcv[1, 0].astype(F32)
        out_ref[...] = screcv[0, 1].astype(F32) + screcv[1, 1].astype(F32)

        @pl.when(jnp.logical_not(alone))
        def _():
            desc(scsend.at[0], scsend.at[0], LABEL("sc", 0), 0, from_dev[0]).wait_send()

        desc(scsend.at[0], scsend.at[0], LABEL("sc", 1), 0, from_dev[1]).wait_send()

    for arr in (0, 1):
        zstep(2, arr)
    for k in (1, -1, 2):
        arrive(wall.at[xat(-k)], "w", k)
    for k in (1, 2, 3):
        arrive(dh.at[yat(-k)], "dh", k)
    eterm(0)
    for arr in (0, 1):
        zstep(3, arr)
    eterm(1)
    for arr in (0, 1):
        zstep(4, arr)
    other(0)
    grads(0)
    other(1)
    grads(1)
    zadd(1)
    yterm(0)
    yterm(1)
    grads2(0)
    grads2(1)
    zadd(2)
    gather_y(0, 1)
    gather_x(0, 0)
    gather_y(1, 1)
    gather_x(1, 0)
    zadd(3)
    gather_y(0, 2)
    gather_y(0, 3)
    gather_x(0, 1)
    gather_y(1, 2)
    gather_y(1, 3)
    gather_x(1, 1)
    zadd(4)
    gather_x(0, 2)
    gather_x(0, 3)
    zend()
    scatter()
    gather_x(1, 2)
    gather_x(1, 3)
    total = ykeep[yl]
    for k in (1, 2, 3):
        for arr, (lo, n) in enumerate(PARTS):
            arrive(yrecv.at[k - 1, pl.ds(lo, n)], "y", arr, k)
        total = total + yrecv[k - 1].astype(F32)
    qkv_ref[...] = total[0:QF]
    gat_ref[...] = total[QF:QO].T
    scatter_end()
    for p in (0, 1):
        for j in range(4):
            gather_end(p, j)
    for row in range(16):
        gwq_ref[:, row * 256:(row + 1) * 256] = gout[row, 0:QF]
        gwo_ref[:, row * 256:(row + 1) * 256] = gout[row, QF:QO]
    turn_sent(0)
    turn_sent(1)
    for cp in sent:
        cp.wait_send()


def spread(*refs):
    n = len(refs) // 2
    copies = [pltpu.make_async_copy(refs[i], refs[n + i], refs[2 * n].at[i]) for i in range(n)]
    for cp in copies:
        cp.start()
    for cp in copies:
        cp.wait()


def shards(x_store, attn_store, replay_idx, w_qkv, w_out, d_qkv, d_out):
    vm, hbm = pl.BlockSpec(memory_space=pltpu.VMEM), pl.BlockSpec(memory_space=pl.ANY)
    shapes = [((QF, ROWS), F32), ((ROWS, 128), F32), ((ROWS, 128), F32), ((ROWS, 128), F32),
              ((QF, 4096), BF), ((OF, 4096), BF)]
    scratch = [
        ((ROWS, 128), BF),
        ((ROWS, 128), BF),
        ((1, ROWS), jnp.int32),
        ((2, ROWS, 128), BF),
        ((4, QO, ROWS), BF),
        ((4, QO, 256), BF),
        ((2, 2, 8, 256, 128), BF),
        ((3, QO, 256), BF),
        ((QO, 256), F32),
        ((3, QO, 256), BF),
        ((16, QO, 256), BF),
        ((4, QO, ROWS), BF),
        ((3, QO, ROWS), BF),
        ((4, QO, ROWS), F32),
        ((2, 8, 256, 128), BF),
        ((2, 8, 256, 128), BF),
        ((2, 8, 256, 128), F32),
        ((2, 2, 4, 256, 128), BF),
        ((2, 2, 4, 256, 128), BF),
        ((2, 2, ROWS, 128), BF),
        ((2, 2, ROWS, 128), BF),
    ]
    count = 200
    parts = pl.pallas_call(
        kernel,
        name="critic_layer",
        out_shape=[jax.ShapeDtypeStruct(s, d) for s, d in shapes],
        in_specs=[hbm] * 7,
        out_specs=[vm] * 6,
        scratch_shapes=[pltpu.VMEM(s, d) for s, d in scratch]
        + [pltpu.SemaphoreType.DMA((n,)) for n in (count, count, 7)],
        compiler_params=pltpu.CompilerParams(
            collective_id=0, has_side_effects=True, vmem_limit_bytes=48 << 20),
    )(*(pltpu.with_memory_space_constraint(v, pltpu.HBM)
        for v in (x_store, attn_store, replay_idx, w_qkv, w_out, d_qkv.T, d_out)))
    qkv, *rest = pl.pallas_call(
        spread,
        name="spread",
        out_shape=[jax.ShapeDtypeStruct(s, d) for s, d in shapes],
        in_specs=[hbm] * 6,
        out_specs=[hbm] * 6,
        scratch_shapes=[pltpu.SemaphoreType.DMA((6,))],
        compiler_params=pltpu.CompilerParams(vmem_limit_bytes=1 << 20),
    )(*parts)
    return (qkv.T, *rest)


def solution(mesh):
    in_specs = (
        P("replay", "tensor"),
        P("replay", "tensor"),
        P("replay", None),
        P("tensor", "replay"),
        P("tensor", "replay"),
        P("replay", "tensor"),
        P("replay", "tensor"),
    )
    out_specs = (
        P("replay", "tensor"),
        P("replay", "tensor"),
        P("replay", "tensor"),
        P("replay", "tensor"),
        P("tensor", None),
        P("tensor", None),
    )
    return jax.shard_map(shards, mesh=mesh, in_specs=in_specs, out_specs=out_specs, check_vma=False)
```

```python
import jax
import jax.numpy as jnp
from jax import lax
from jax.experimental import pallas as pl
from jax.experimental.pallas import tpu as pltpu
from jax.sharding import PartitionSpec as P

BF, F32 = jnp.bfloat16, jnp.float32
MESH = pl.DeviceIdType.MESH
ROWS, QF, OF, QO = 128, 192, 128, 320
PARTS = ((0, QF), (QF, OF))
PIECES = ((0, 96), (96, 96), (192, 64), (256, 64))


def dot(a, b, ca, cb):
    return lax.dot_general(a, b, (((ca,), (cb,)), ((), ())), preferred_element_type=F32)


def make_labels():
    table = {}

    def label(*key):
        return table.setdefault(key, len(table))

    return table, label


TABLE, LABEL = make_labels()


def kernel(x_ref, a_ref, idx_ref, wq_ref, wo_ref, dq_ref, do_ref,
           qkv_ref, out_ref, gin_ref, gat_ref, gwq_ref, gwo_ref,
           xin, ain, idx, own, dh, wall, xb, gsend, gkeep, gr, gout,
           ysend, yrecv, ykeep, esend, erecv, part, zsend, zrecv, scsend, screcv,
           ssem, rsem, lsem):
    t, r = lax.axis_index("tensor"), lax.axis_index("replay")
    c, yh, z = lax.rem(t, 2), lax.rem(t // 2, 2), t // 4
    x, yl = r // 4, lax.rem(r, 4)
    h = lax.rem(z, 2)

    def device(x_, yl_, yh_, z_, c_):
        return ((z_ * 2 + yh_) * 2 + c_, x_ * 4 + yl_)

    def xat(k):
        return lax.rem(x + k + 4, 4)

    def yat(k):
        return lax.rem(yl + k + 4, 4)

    def zat(k):
        return lax.rem(z + k + 8, 8)

    xdev = {k: device(xat(k), yl, yh, z, c) for k in (1, -1, 2)}
    zdev = {k: device(x, yl, yh, zat(k), c) for k in (1, -1)}
    ydev = {k: device(x, yat(k), yh, z, c) for k in (1, 2, 3)}
    sib = device(x, yl, yh, z, 1 - c)
    q = 2 * h + yh
    zt = 2 * (z // 2) + yl // 2
    alone = yl == q
    yhs = (yh, 1 - yh)
    to_dev = [device(x, q, v, zt, c) for v in yhs]
    from_dev = [device(x, 2 * h + v, lax.rem(yl, 2), zt, c) for v in yhs]

    loads = [
        pltpu.make_async_copy(src, dst, lsem.at[i])
        for i, (src, dst) in enumerate((
            (idx_ref, idx), (x_ref, xin), (do_ref, own.at[1]),
            (wq_ref, wall.at[x, pl.ds(0, QF)]), (wo_ref, wall.at[x, pl.ds(QF, OF)]),
            (dq_ref, dh.at[yl, pl.ds(0, QF)]), (a_ref, ain)))
    ]
    for cp in loads:
        cp.start()

    bar = pltpu.get_barrier_semaphore()
    peers = list(xdev.values()) + list(zdev.values()) + list(ydev.values()) + [sib]
    for d in peers + to_dev + from_dev:
        pl.semaphore_signal(bar, inc=1, device_id=d, device_id_type=MESH)

    sent = []
    near = jnp.where(yl == 0, 3, 1)
    slot_y = (yl, yat(2), yat(-near), yat(near))
    inner = jnp.logical_and(yl > 0, yl < 3)
    end = 3 * (yl // 2)
    ends = []

    def desc(src, dst, s, rs, dev):
        return pltpu.make_async_remote_copy(
            src_ref=src, dst_ref=dst, send_sem=ssem.at[s], recv_sem=rsem.at[rs],
            device_id=dev, device_id_type=MESH)

    def send(src, dst, dev, *key):
        s = LABEL(*key)
        cp = desc(src, dst, s, s, dev)
        cp.start()
        sent.append(cp)

    def arrive(dst, *key):
        s = LABEL(*key)
        desc(dst, dst, s, s, sib).wait_recv()

    iota0 = lax.broadcasted_iota(jnp.int32, (ROWS, ROWS), 0)
    loads[0].wait()
    loads[1].wait()
    pick = jnp.where(iota0 == idx[...], 1.0, 0.0).astype(BF)
    own[0] = dot(pick, xin[...], 0, 0).astype(BF)
    for cp in loads[2:]:
        cp.wait()
    dh[yl, QF:QO] = dot(ain[...], pick, 0, 0).astype(BF)
    pl.semaphore_wait(bar, len(peers) + 4)

    def line(block, *key):
        first = LABEL(*key, 1)
        assert (LABEL(*key, 2), LABEL(*key, 3)) == (first + 1, first + 2)

        def go(k, slot):
            s = LABEL(*key, "k", k)
            return desc(block(yl), block(yl), s, first + slot - 1, ydev[k])

        go(2, 1).start()
        pl.when(yl != 3)(lambda: go(1, 2).start())
        pl.when(yl != 0)(lambda: go(3, jnp.where(yl == 1, 2, 3)).start())
        ends.append(lambda: go(2, 1).wait_send())
        ends.append(lambda: pl.when(yl != 3)(lambda: go(1, 2).wait_send()))
        ends.append(lambda: pl.when(yl != 0)(lambda: go(3, 3).wait_send()))

    def line_take(block, slot, *key):
        arrive(block(slot_y[slot]), *key, slot)
        if slot == 1:
            s = LABEL(*key, "k", 0)

            def go():
                return desc(block(yat(2)), block(yat(2)), s, LABEL(*key, 3), device(x, end, yh, z, c))

            pl.when(inner)(lambda: go().start())
            ends.append(lambda: pl.when(inner)(lambda: go().wait_send()))

    def turn(arr):
        dst = xb.at[arr, c, zt, pl.ds(pl.multiple_of(lax.rem(yl, 2) * ROWS, ROWS), ROWS)]
        rs = LABEL("turn", arr, 0) + lax.rem(yl, 2)
        assert LABEL("turn", arr, 1) == LABEL("turn", arr, 0) + 1

        @pl.when(alone)
        def _():
            pltpu.make_async_copy(own.at[arr], dst, rsem.at[rs]).start()

        @pl.when(jnp.logical_not(alone))
        def _():
            desc(own.at[arr], dst, LABEL("turn", arr, 0), rs, to_dev[0]).start()

        desc(own.at[arr], dst, LABEL("turn", arr, 1), rs, to_dev[1]).start()

    def turn_sent(arr):
        @pl.when(jnp.logical_not(alone))
        def _():
            desc(own.at[arr], own.at[arr], LABEL("turn", arr, 0), 0, to_dev[0]).wait_send()

        desc(own.at[arr], own.at[arr], LABEL("turn", arr, 1), 0, to_dev[1]).wait_send()

    turn(0)
    turn(1)
    for k in (1, -1, 2):
        send(wall.at[x], wall.at[x], xdev[k], "w", k)

    def zways(step, arr):
        return [w for w in (1, -1) if step < 4 or (arr == 0) == (w == 1)]

    def zblock(core, step, arr, way, v):
        return xb.at[arr, core, zat(-way * step), pl.ds(v * ROWS, ROWS)]

    def zpass(step, arr, way, v):
        if way in zways(step, arr):
            piece = zblock(c, step - 1, arr, way, v)
            send(piece, piece, zdev[way], "z", step, arr, way, v)

    def zgive(step, arr, way, v):
        piece = zblock(c, step, arr, way, v)
        send(piece, piece, sib, "s", step, arr, way, v)

    def zfirst(arr):
        for v in (0, 1):
            arrive(zblock(c, 0, arr, 1, v), "turn", arr, v)
            for way in (1, -1):
                zpass(1, arr, way, v)
        for v in (0, 1):
            zgive(0, arr, 1, v)

    def zstep(step, arr):
        for v in (0, 1):
            for way in zways(step, arr):
                arrive(zblock(c, step, arr, way, v), "z", step, arr, way, v)
                if step < 4:
                    zpass(step + 1, arr, way, v)
        for v in (0, 1):
            for way in zways(step, arr):
                zgive(step, arr, way, v)

    def other(arr):
        for v in (0, 1):
            arrive(zblock(1 - c, 0, arr, 1, v), "s", 0, arr, 1, v)
        for step in (1, 2, 3, 4):
            for v in (0, 1):
                for way in zways(step, arr):
                    arrive(zblock(1 - c, step, arr, way, v), "s", step, arr, way, v)

    def block(arr, xp):
        return jnp.concatenate(
            [jnp.concatenate([xb[arr, 0, 2 * xp + v], xb[arr, 1, 2 * xp + v]], axis=1) for v in (0, 1)], axis=0)

    def grads(p):
        lo, n = PARTS[p]
        lhs = jnp.concatenate([dh[g, lo:lo + n] for g in range(4)], axis=1)

        def term(k):
            return dot(lhs, block(p, xat(k)), 1, 0) * (1.0 / ROWS)

        for i, k in enumerate((2, 1, -1)):
            gsend[i, lo:lo + n] = term(k).astype(BF)
            send(gsend.at[i, pl.ds(lo, n)], gr.at[i, pl.ds(lo, n)], xdev[k], "g", p, k)
        gkeep[lo:lo + n] = term(0)

    def grads2(p):
        lo, n = PARTS[p]
        total = gkeep[lo:lo + n]
        for i, k in enumerate((2, 1, -1)):
            arrive(gr.at[i, pl.ds(lo, n)], "g", p, k)
            total = total + gr[i, lo:lo + n].astype(F32)
        gout[r, lo:lo + n] = total.astype(BF)
        for piece in (2 * p, 2 * p + 1):
            lo, n = PIECES[piece]
            mine = gout.at[r, pl.ds(lo, n)]
            for k in (1, -1):
                send(mine, mine, xdev[k], "ax", piece, 0, k)
            line(lambda y: gout.at[x * 4 + y, pl.ds(lo, n)], "ay", piece)

    def gather_y(p, *slots):
        lo, n = PIECES[p]
        for slot in slots:
            line_take(lambda y: gout.at[x * 4 + y, pl.ds(lo, n)], slot, "ay", p)
            piece = gout.at[x * 4 + slot_y[slot], pl.ds(lo, n)]
            for k in (1, -1):
                send(piece, piece, xdev[k], "ax", p, slot, k)

    def gather_x(p, *slots):
        lo, n = PIECES[p]
        half = n // 2
        for slot in slots:
            for k, at in ((1, lo), (-1, lo + half)):
                row = xat(-k) * 4 + slot_y[slot]
                arrive(gout.at[row, pl.ds(lo, n)], "ax", p, slot, k)
                piece = gout.at[row, pl.ds(at, half)]
                send(piece, piece, xdev[k], "ar", p, slot, k)

    def gather_end(p):
        lo, n = PIECES[p]
        half = n // 2
        for slot in range(4):
            for k, at in ((1, lo), (-1, lo + half)):
                arrive(gout.at[xat(2) * 4 + slot_y[slot], pl.ds(at, half)], "ar", p, slot, k)

    def eterm(arr):
        lo, n = PARTS[arr]
        w = jnp.concatenate([wall[v, lo:lo + n] for v in range(4)], axis=1)
        for g in range(4):
            y = dot(dh[g, lo:lo + n], w, 0, 0)
            rows = slice(g % 2 * ROWS, g % 2 * ROWS + ROWS)
            for xp in range(4):
                left, right = y[:, xp * 256:xp * 256 + 128], y[:, xp * 256 + 128:xp * 256 + 256]
                part[arr, 2 * xp + g // 2, rows] = jnp.where(c == 0, left, right)
                esend[arr, 2 * xp + g // 2, rows] = jnp.where(c == 0, right, left).astype(BF)
        send(esend.at[arr], erecv.at[arr], sib, "e", arr)

    def yterm(arr):
        lo, n = PARTS[arr]
        w = jnp.concatenate([wall[v, lo:lo + n] for v in range(4)], axis=1)
        for v in (0, 1):
            rhs = jnp.concatenate([xb[arr, cc, 2 * xp + v] for xp in range(4) for cc in (0, 1)], axis=1)
            y = dot(w, rhs, 1, 1)
            for j in (0, 1):
                ykeep[2 * v + j, lo:lo + n] = y[:, j * ROWS:(j + 1) * ROWS]
                ysend[2 * v + j, lo:lo + n] = y[:, j * ROWS:(j + 1) * ROWS].astype(BF)

    def ygo(arr):
        lo, n = PARTS[arr]
        for k in (1, 2, 3):
            send(ysend.at[yat(k), pl.ds(lo, n)], yrecv.at[k - 1, pl.ds(lo, n)], ydev[k], "y", arr, k)

    def zadd(step):
        for arr in (0, 1):
            if step == 1:
                arrive(erecv.at[arr], "e", arr)
                for v in range(8):
                    part[arr, v] = part[arr, v] + erecv[arr, v].astype(F32)
            for way in (1, -1):
                i = (1 - way) // 2
                if step == 1 and (arr == 0) != (way == 1):
                    continue
                at = zat(way * (5 - step))
                value = part[arr, at]
                if step > 2 or (step == 2 and (arr == 0) == (way == 1)):
                    arrive(zrecv.at[arr, i, step - 2], "r", step - 1, arr, way)
                    value = value + zrecv[arr, i, step - 2].astype(F32)
                zsend[arr, i, step - 1] = value.astype(BF)
                send(zsend.at[arr, i, step - 1], zrecv.at[arr, i, step - 1], zdev[way], "r", step, arr, way)

    def zend():
        for arr in (0, 1):
            value = part[arr, z]
            for way in (1, -1):
                i = (1 - way) // 2
                arrive(zrecv.at[arr, i, 3], "r", 4, arr, way)
                value = value + zrecv[arr, i, 3].astype(F32)
            value = value.astype(BF)
            for j in (0, 1):
                scsend[j, arr] = value[j * ROWS:(j + 1) * ROWS]

    def scatter():
        rs = LABEL("sc", 0) + yh
        assert LABEL("sc", 1) == LABEL("sc", 0) + 1
        dst = screcv.at[yh]

        @pl.when(alone)
        def _():
            pltpu.make_async_copy(scsend.at[yhs[0]], dst, rsem.at[rs]).start()

        @pl.when(jnp.logical_not(alone))
        def _():
            desc(scsend.at[yhs[0]], dst, LABEL("sc", 0), rs, from_dev[0]).start()

        desc(scsend.at[yhs[1]], dst, LABEL("sc", 1), rs, from_dev[1]).start()

    def scatter_end():
        for v in (0, 1):
            arrive(screcv.at[v], "sc", v)
        gin_ref[...] = screcv[0, 0].astype(F32) + screcv[1, 0].astype(F32)
        out_ref[...] = screcv[0, 1].astype(F32) + screcv[1, 1].astype(F32)

        @pl.when(jnp.logical_not(alone))
        def _():
            desc(scsend.at[0], scsend.at[0], LABEL("sc", 0), 0, from_dev[0]).wait_send()

        desc(scsend.at[0], scsend.at[0], LABEL("sc", 1), 0, from_dev[1]).wait_send()

    def dhblock(y):
        return dh.at[y]

    zfirst(0)
    line(dhblock, "dh")
    zfirst(1)
    for arr in (0, 1):
        zstep(1, arr)
    for arr in (0, 1):
        zstep(2, arr)
    line_take(dhblock, 1, "dh")
    for arr in (0, 1):
        zstep(3, arr)
    line_take(dhblock, 2, "dh")
    line_take(dhblock, 3, "dh")
    zstep(4, 0)
    other(0)
    grads(0)
    zstep(4, 1)
    other(1)
    grads(1)
    for k in (1, -1, 2):
        arrive(wall.at[xat(-k)], "w", k)
    eterm(0)
    eterm(1)
    yterm(0)
    ygo(0)
    yterm(1)
    zadd(1)
    grads2(0)
    grads2(1)
    zadd(2)
    gather_x(0, 0)
    gather_y(0, 1, 2, 3)
    gather_x(1, 0)
    gather_y(1, 1, 2, 3)
    zadd(3)
    gather_x(0, 1, 2, 3)
    gather_x(2, 0)
    gather_y(2, 1, 2, 3)
    gather_x(1, 1, 2, 3)
    gather_x(3, 0)
    gather_y(3, 1, 2, 3)
    zadd(4)
    ygo(1)
    gather_x(2, 1, 2, 3)
    zend()
    scatter()
    gather_x(3, 1, 2, 3)
    total = ykeep[yl]
    for k in (1, 2, 3):
        for arr, (lo, n) in enumerate(PARTS):
            arrive(yrecv.at[k - 1, pl.ds(lo, n)], "y", arr, k)
        total = total + yrecv[k - 1].astype(F32)
    qkv_ref[...] = total[0:QF]
    gat_ref[...] = total[QF:QO].T
    scatter_end()
    for p in range(4):
        gather_end(p)
    for row in range(16):
        gwq_ref[:, row * 256:(row + 1) * 256] = gout[row, 0:QF]
        gwo_ref[:, row * 256:(row + 1) * 256] = gout[row, QF:QO]
    turn_sent(0)
    turn_sent(1)
    for cp in sent:
        cp.wait_send()
    for wait in ends:
        wait()


def spread(*refs):
    n = len(refs) // 2
    copies = [pltpu.make_async_copy(refs[i], refs[n + i], refs[2 * n].at[i]) for i in range(n)]
    for cp in copies:
        cp.start()
    for cp in copies:
        cp.wait()


def shards(x_store, attn_store, replay_idx, w_qkv, w_out, d_qkv, d_out):
    vm, hbm = pl.BlockSpec(memory_space=pltpu.VMEM), pl.BlockSpec(memory_space=pl.ANY)
    shapes = [((QF, ROWS), F32), ((ROWS, 128), F32), ((ROWS, 128), F32), ((ROWS, 128), F32),
              ((QF, 4096), BF), ((OF, 4096), BF)]
    scratch = [
        ((ROWS, 128), BF),
        ((ROWS, 128), BF),
        ((1, ROWS), jnp.int32),
        ((2, ROWS, 128), BF),
        ((4, QO, ROWS), BF),
        ((4, QO, 256), BF),
        ((2, 2, 8, 256, 128), BF),
        ((3, QO, 256), BF),
        ((QO, 256), F32),
        ((3, QO, 256), BF),
        ((16, QO, 256), BF),
        ((4, QO, ROWS), BF),
        ((3, QO, ROWS), BF),
        ((4, QO, ROWS), F32),
        ((2, 8, 256, 128), BF),
        ((2, 8, 256, 128), BF),
        ((2, 8, 256, 128), F32),
        ((2, 2, 4, 256, 128), BF),
        ((2, 2, 4, 256, 128), BF),
        ((2, 2, ROWS, 128), BF),
        ((2, 2, ROWS, 128), BF),
    ]
    count = 240
    parts = pl.pallas_call(
        kernel,
        name="critic_layer",
        out_shape=[jax.ShapeDtypeStruct(s, d) for s, d in shapes],
        in_specs=[hbm] * 7,
        out_specs=[vm] * 6,
        scratch_shapes=[pltpu.VMEM(s, d) for s, d in scratch]
        + [pltpu.SemaphoreType.DMA((n,)) for n in (count, count, 7)],
        compiler_params=pltpu.CompilerParams(
            collective_id=0, has_side_effects=True, vmem_limit_bytes=48 << 20),
    )(*(pltpu.with_memory_space_constraint(v, pltpu.HBM)
        for v in (x_store, attn_store, replay_idx, w_qkv, w_out, d_qkv.T, d_out)))
    qkv, *rest = pl.pallas_call(
        spread,
        name="spread",
        out_shape=[jax.ShapeDtypeStruct(s, d) for s, d in shapes],
        in_specs=[hbm] * 6,
        out_specs=[hbm] * 6,
        scratch_shapes=[pltpu.SemaphoreType.DMA((6,))],
        compiler_params=pltpu.CompilerParams(vmem_limit_bytes=1 << 20),
    )(*parts)
    return (qkv.T, *rest)


def solution(mesh):
    in_specs = (
        P("replay", "tensor"),
        P("replay", "tensor"),
        P("replay", None),
        P("tensor", "replay"),
        P("tensor", "replay"),
        P("replay", "tensor"),
        P("replay", "tensor"),
    )
    out_specs = (
        P("replay", "tensor"),
        P("replay", "tensor"),
        P("replay", "tensor"),
        P("replay", "tensor"),
        P("tensor", None),
        P("tensor", None),
    )
    return jax.shard_map(shards, mesh=mesh, in_specs=in_specs, out_specs=out_specs, check_vma=False)
```

```python
import jax
import jax.numpy as jnp
from jax import lax
from jax.experimental import pallas as pl
from jax.experimental.pallas import tpu as pltpu
from jax.sharding import PartitionSpec as P

BF, F32 = jnp.bfloat16, jnp.float32
MESH = pl.DeviceIdType.MESH
ROWS, QF, OF, QO = 128, 192, 128, 320
PARTS = ((0, QF), (QF, OF))
PIECES = ((0, 96), (96, 96), (192, 64), (256, 64))


def dot(a, b, ca, cb):
    return lax.dot_general(a, b, (((ca,), (cb,)), ((), ())), preferred_element_type=F32)


def make_labels():
    table = {}

    def label(*key):
        return table.setdefault(key, len(table))

    return table, label


TABLE, LABEL = make_labels()


def kernel(x_ref, a_ref, idx_ref, wq_ref, wo_ref, dq_ref, do_ref,
           qkv_ref, out_ref, gin_ref, gat_ref, gwq_ref, gwo_ref,
           xin, ain, idx, own, dh, wall, xb, gsend, gkeep, gr, gout,
           ysend, yrecv, ykeep, esend, erecv, part, zsend, zrecv, scsend, screcv,
           ssem, rsem, lsem):
    t, r = lax.axis_index("tensor"), lax.axis_index("replay")
    c, yh, z = lax.rem(t, 2), lax.rem(t // 2, 2), t // 4
    x, yl = r // 4, lax.rem(r, 4)
    h = lax.rem(z, 2)

    def device(x_, yl_, yh_, z_, c_):
        return ((z_ * 2 + yh_) * 2 + c_, x_ * 4 + yl_)

    def xat(k):
        return lax.rem(x + k + 4, 4)

    def yat(k):
        return lax.rem(yl + k + 4, 4)

    def zat(k):
        return lax.rem(z + k + 8, 8)

    xdev = {k: device(xat(k), yl, yh, z, c) for k in (1, -1, 2)}
    zdev = {k: device(x, yl, yh, zat(k), c) for k in (1, -1)}
    ydev = {k: device(x, yat(k), yh, z, c) for k in (1, 2, 3)}
    sib = device(x, yl, yh, z, 1 - c)
    q = 2 * h + yh
    zt = 2 * (z // 2) + yl // 2
    alone = yl == q
    yhs = (yh, 1 - yh)
    to_dev = [device(x, q, v, zt, c) for v in yhs]
    from_dev = [device(x, 2 * h + v, lax.rem(yl, 2), zt, c) for v in yhs]

    loads = [
        pltpu.make_async_copy(src, dst, lsem.at[i])
        for i, (src, dst) in enumerate((
            (idx_ref, idx), (x_ref, xin), (do_ref, own.at[1]),
            (wq_ref, wall.at[x, pl.ds(0, QF)]), (wo_ref, wall.at[x, pl.ds(QF, OF)]),
            (dq_ref, dh.at[yl, pl.ds(0, QF)]), (a_ref, ain)))
    ]
    for cp in loads:
        cp.start()

    bar = pltpu.get_barrier_semaphore()
    peers = list(xdev.values()) + list(zdev.values()) + list(ydev.values()) + [sib]
    for d in peers + to_dev + from_dev:
        pl.semaphore_signal(bar, inc=1, device_id=d, device_id_type=MESH)

    sent = []
    near = jnp.where(yl == 0, 3, 1)
    slot_y = (yl, yat(2), yat(-near), yat(near))
    inner = jnp.logical_and(yl > 0, yl < 3)
    end = 3 * (yl // 2)
    ends = []

    def desc(src, dst, s, rs, dev):
        return pltpu.make_async_remote_copy(
            src_ref=src, dst_ref=dst, send_sem=ssem.at[s], recv_sem=rsem.at[rs],
            device_id=dev, device_id_type=MESH)

    def send(src, dst, dev, *key):
        s = LABEL(*key)
        cp = desc(src, dst, s, s, dev)
        cp.start()
        sent.append(cp)

    def arrive(dst, *key):
        s = LABEL(*key)
        desc(dst, dst, s, s, sib).wait_recv()

    iota0 = lax.broadcasted_iota(jnp.int32, (ROWS, ROWS), 0)
    loads[0].wait()
    loads[1].wait()
    pick = jnp.where(iota0 == idx[...], 1.0, 0.0).astype(BF)
    own[0] = dot(pick, xin[...], 0, 0).astype(BF)
    pl.semaphore_wait(bar, len(peers) + 4)

    def line(block, *key):
        first = LABEL(*key, 1)
        assert (LABEL(*key, 2), LABEL(*key, 3)) == (first + 1, first + 2)

        def go(k, slot):
            s = LABEL(*key, "k", k)
            return desc(block(yl), block(yl), s, first + slot - 1, ydev[k])

        go(2, 1).start()
        pl.when(yl != 3)(lambda: go(1, 2).start())
        pl.when(yl != 0)(lambda: go(3, jnp.where(yl == 1, 2, 3)).start())
        ends.append(lambda: go(2, 1).wait_send())
        ends.append(lambda: pl.when(yl != 3)(lambda: go(1, 2).wait_send()))
        ends.append(lambda: pl.when(yl != 0)(lambda: go(3, 3).wait_send()))

    def line_take(block, slot, *key):
        arrive(block(slot_y[slot]), *key, slot)
        if slot == 1:
            s = LABEL(*key, "k", 0)

            def go():
                return desc(block(yat(2)), block(yat(2)), s, LABEL(*key, 3), device(x, end, yh, z, c))

            pl.when(inner)(lambda: go().start())
            ends.append(lambda: pl.when(inner)(lambda: go().wait_send()))

    def turn(arr):
        dst = xb.at[arr, c, zt, pl.ds(pl.multiple_of(lax.rem(yl, 2) * ROWS, ROWS), ROWS)]
        rs = LABEL("turn", arr, 0) + lax.rem(yl, 2)
        assert LABEL("turn", arr, 1) == LABEL("turn", arr, 0) + 1

        @pl.when(alone)
        def _():
            pltpu.make_async_copy(own.at[arr], dst, rsem.at[rs]).start()

        @pl.when(jnp.logical_not(alone))
        def _():
            desc(own.at[arr], dst, LABEL("turn", arr, 0), rs, to_dev[0]).start()

        desc(own.at[arr], dst, LABEL("turn", arr, 1), rs, to_dev[1]).start()

    def turn_sent(arr):
        @pl.when(jnp.logical_not(alone))
        def _():
            desc(own.at[arr], own.at[arr], LABEL("turn", arr, 0), 0, to_dev[0]).wait_send()

        desc(own.at[arr], own.at[arr], LABEL("turn", arr, 1), 0, to_dev[1]).wait_send()

    turn(0)
    for cp in loads[2:]:
        cp.wait()
    turn(1)
    dh[yl, QF:QO] = dot(ain[...], pick, 0, 0).astype(BF)
    for k in (1, -1, 2):
        send(wall.at[x], wall.at[x], xdev[k], "w", k)

    def zways(step, arr):
        return [w for w in (1, -1) if step < 4 or (arr == 0) == (w == 1)]

    def zblock(core, step, arr, way, v):
        if v is None:
            return xb.at[arr, core, zat(-way * step)]
        return xb.at[arr, core, zat(-way * step), pl.ds(v * ROWS, ROWS)]

    def zpass(step, arr, way, v):
        if way in zways(step, arr):
            piece = zblock(c, step - 1, arr, way, v)
            send(piece, piece, zdev[way], "z", step, arr, way, v)

    def zgive(step, arr, way, v):
        piece = zblock(c, step, arr, way, v)
        send(piece, piece, sib, "s", step, arr, way, v)

    def zfirst(arr):
        for v in (0, 1):
            arrive(zblock(c, 0, arr, 1, v), "turn", arr, v)
        for way in (1, -1):
            zpass(1, arr, way, None)
        zgive(0, arr, 1, None)

    def zstep(step, arr):
        for way in zways(step, arr):
            arrive(zblock(c, step, arr, way, None), "z", step, arr, way, None)
            if step < 4:
                zpass(step + 1, arr, way, None)
        for way in zways(step, arr):
            zgive(step, arr, way, None)

    def other(arr):
        arrive(zblock(1 - c, 0, arr, 1, None), "s", 0, arr, 1, None)
        for step in (1, 2, 3, 4):
            for way in zways(step, arr):
                arrive(zblock(1 - c, step, arr, way, None), "s", step, arr, way, None)

    def block(arr, xp):
        return jnp.concatenate(
            [jnp.concatenate([xb[arr, 0, 2 * xp + v], xb[arr, 1, 2 * xp + v]], axis=1) for v in (0, 1)], axis=0)

    def grads(p):
        lo, n = PARTS[p]
        lhs = jnp.concatenate([dh[g, lo:lo + n] for g in range(4)], axis=1)

        def term(k):
            return dot(lhs, block(p, xat(k)), 1, 0) * (1.0 / ROWS)

        for i, k in enumerate((2, 1, -1)):
            gsend[i, lo:lo + n] = term(k).astype(BF)
            send(gsend.at[i, pl.ds(lo, n)], gr.at[i, pl.ds(lo, n)], xdev[k], "g", p, k)
        gkeep[lo:lo + n] = term(0)

    def grads2(p):
        lo, n = PARTS[p]
        total = gkeep[lo:lo + n]
        for i, k in enumerate((2, 1, -1)):
            arrive(gr.at[i, pl.ds(lo, n)], "g", p, k)
            total = total + gr[i, lo:lo + n].astype(F32)
        gout[r, lo:lo + n] = total.astype(BF)
        for piece in (2 * p, 2 * p + 1):
            lo, n = PIECES[piece]
            mine = gout.at[r, pl.ds(lo, n)]
            for k in (1, -1):
                send(mine, mine, xdev[k], "ax", piece, 0, k)
            line(lambda y: gout.at[x * 4 + y, pl.ds(lo, n)], "ay", piece)

    def gather_y(p, *slots):
        lo, n = PIECES[p]
        for slot in slots:
            line_take(lambda y: gout.at[x * 4 + y, pl.ds(lo, n)], slot, "ay", p)
            piece = gout.at[x * 4 + slot_y[slot], pl.ds(lo, n)]
            for k in (1, -1):
                send(piece, piece, xdev[k], "ax", p, slot, k)

    def gather_x(p, *slots):
        lo, n = PIECES[p]
        half = n // 2
        for slot in slots:
            for k, at in ((1, lo), (-1, lo + half)):
                row = xat(-k) * 4 + slot_y[slot]
                arrive(gout.at[row, pl.ds(lo, n)], "ax", p, slot, k)
                piece = gout.at[row, pl.ds(at, half)]
                send(piece, piece, xdev[k], "ar", p, slot, k)

    def put(k):
        for y in range(4):
            row = xat(k) * 4 + y
            cols = pl.ds(pl.multiple_of(row * 256, 256), 256)
            gwq_ref[:, cols] = gout[row, 0:QF]
            gwo_ref[:, cols] = gout[row, QF:QO]

    def gather_end(p):
        lo, n = PIECES[p]
        half = n // 2
        for slot in range(4):
            for k, at in ((1, lo), (-1, lo + half)):
                arrive(gout.at[xat(2) * 4 + slot_y[slot], pl.ds(at, half)], "ar", p, slot, k)

    def eterm(arr):
        lo, n = PARTS[arr]
        w = jnp.concatenate([wall[v, lo:lo + n] for v in range(4)], axis=1)
        for g in range(4):
            y = dot(dh[g, lo:lo + n], w, 0, 0)
            rows = slice(g % 2 * ROWS, g % 2 * ROWS + ROWS)
            for xp in range(4):
                left, right = y[:, xp * 256:xp * 256 + 128], y[:, xp * 256 + 128:xp * 256 + 256]
                part[arr, 2 * xp + g // 2, rows] = jnp.where(c == 0, left, right)
                esend[arr, 2 * xp + g // 2, rows] = jnp.where(c == 0, right, left).astype(BF)
        send(esend.at[arr], erecv.at[arr], sib, "e", arr)

    def yterm(arr):
        lo, n = PARTS[arr]
        w = jnp.concatenate([wall[v, lo:lo + n] for v in range(4)], axis=1)
        for v in (0, 1):
            rhs = jnp.concatenate([xb[arr, cc, 2 * xp + v] for xp in range(4) for cc in (0, 1)], axis=1)
            y = dot(w, rhs, 1, 1)
            for j in (0, 1):
                ykeep[2 * v + j, lo:lo + n] = y[:, j * ROWS:(j + 1) * ROWS]
                ysend[2 * v + j, lo:lo + n] = y[:, j * ROWS:(j + 1) * ROWS].astype(BF)

    def ygo(arr):
        lo, n = PARTS[arr]
        for k in (1, 2, 3):
            send(ysend.at[yat(k), pl.ds(lo, n)], yrecv.at[k - 1, pl.ds(lo, n)], ydev[k], "y", arr, k)

    def zadd(step):
        for arr in (0, 1):
            if step == 1:
                arrive(erecv.at[arr], "e", arr)
                for v in range(8):
                    part[arr, v] = part[arr, v] + erecv[arr, v].astype(F32)
            for way in (1, -1):
                i = (1 - way) // 2
                if step == 1 and (arr == 0) != (way == 1):
                    continue
                at = zat(way * (5 - step))
                value = part[arr, at]
                if step > 2 or (step == 2 and (arr == 0) == (way == 1)):
                    arrive(zrecv.at[arr, i, step - 2], "r", step - 1, arr, way)
                    value = value + zrecv[arr, i, step - 2].astype(F32)
                zsend[arr, i, step - 1] = value.astype(BF)
                send(zsend.at[arr, i, step - 1], zrecv.at[arr, i, step - 1], zdev[way], "r", step, arr, way)

    def zend():
        for arr in (0, 1):
            value = part[arr, z]
            for way in (1, -1):
                i = (1 - way) // 2
                arrive(zrecv.at[arr, i, 3], "r", 4, arr, way)
                value = value + zrecv[arr, i, 3].astype(F32)
            value = value.astype(BF)
            for j in (0, 1):
                scsend[j, arr] = value[j * ROWS:(j + 1) * ROWS]

    def scatter():
        rs = LABEL("sc", 0) + yh
        assert LABEL("sc", 1) == LABEL("sc", 0) + 1
        dst = screcv.at[yh]

        @pl.when(alone)
        def _():
            pltpu.make_async_copy(scsend.at[yhs[0]], dst, rsem.at[rs]).start()

        @pl.when(jnp.logical_not(alone))
        def _():
            desc(scsend.at[yhs[0]], dst, LABEL("sc", 0), rs, from_dev[0]).start()

        desc(scsend.at[yhs[1]], dst, LABEL("sc", 1), rs, from_dev[1]).start()

    def scatter_end():
        for v in (0, 1):
            arrive(screcv.at[v], "sc", v)
        gin_ref[...] = screcv[0, 0].astype(F32) + screcv[1, 0].astype(F32)
        out_ref[...] = screcv[0, 1].astype(F32) + screcv[1, 1].astype(F32)

        @pl.when(jnp.logical_not(alone))
        def _():
            desc(scsend.at[0], scsend.at[0], LABEL("sc", 0), 0, from_dev[0]).wait_send()

        desc(scsend.at[0], scsend.at[0], LABEL("sc", 1), 0, from_dev[1]).wait_send()

    def dhblock(y):
        return dh.at[y]

    zfirst(0)
    line(dhblock, "dh")

    zfirst(1)

    for arr in (0, 1):
        zstep(1, arr)

    for arr in (0, 1):
        zstep(2, arr)

    line_take(dhblock, 1, "dh")
    for arr in (0, 1):
        zstep(3, arr)

    line_take(dhblock, 2, "dh")
    line_take(dhblock, 3, "dh")

    for k in (1, -1, 2):
        arrive(wall.at[xat(-k)], "w", k)
    eterm(0)
    zstep(4, 0)
    other(0)

    grads(0)

    eterm(1)
    yterm(0)
    ygo(0)

    zstep(4, 1)
    other(1)
    grads(1)
    yterm(1)
    ygo(1)

    zadd(1)

    grads2(0)

    zadd(2)

    grads2(1)

    gather_x(0, 0)
    gather_y(0, 1, 2, 3)

    zadd(3)
    gather_x(1, 0)
    gather_y(1, 1, 2, 3)

    gather_x(0, 1, 2, 3)
    zadd(4)
    gather_x(2, 0)
    gather_y(2, 1, 2, 3)

    zend()
    scatter()

    gather_x(1, 1, 2, 3)
    gather_x(3, 0)
    gather_y(3, 1, 2, 3)

    gather_x(2, 1, 2, 3)

    put(0)
    gather_x(3, 1, 2, 3)
    put(1)
    put(-1)

    total = ykeep[yl]
    for k in (1, 2, 3):
        for arr, (lo, n) in enumerate(PARTS):
            arrive(yrecv.at[k - 1, pl.ds(lo, n)], "y", arr, k)
        total = total + yrecv[k - 1].astype(F32)
    qkv_ref[...] = total[0:QF]
    gat_ref[...] = total[QF:QO].T

    scatter_end()

    for p in range(4):
        gather_end(p)

    put(2)
    turn_sent(0)
    turn_sent(1)
    for cp in sent:
        cp.wait_send()
    for wait in ends:
        wait()


def spread(*refs):
    n = len(refs) // 2
    copies = [pltpu.make_async_copy(refs[i], refs[n + i], refs[2 * n].at[i]) for i in range(n)]
    for cp in copies:
        cp.start()
    for cp in copies:
        cp.wait()


def shards(x_store, attn_store, replay_idx, w_qkv, w_out, d_qkv, d_out):
    vm, hbm = pl.BlockSpec(memory_space=pltpu.VMEM), pl.BlockSpec(memory_space=pl.ANY)
    shapes = [((QF, ROWS), F32), ((ROWS, 128), F32), ((ROWS, 128), F32), ((ROWS, 128), F32),
              ((QF, 4096), BF), ((OF, 4096), BF)]
    scratch = [
        ((ROWS, 128), BF),
        ((ROWS, 128), BF),
        ((1, ROWS), jnp.int32),
        ((2, ROWS, 128), BF),
        ((4, QO, ROWS), BF),
        ((4, QO, 256), BF),
        ((2, 2, 8, 256, 128), BF),
        ((3, QO, 256), BF),
        ((QO, 256), F32),
        ((3, QO, 256), BF),
        ((16, QO, 256), BF),
        ((4, QO, ROWS), BF),
        ((3, QO, ROWS), BF),
        ((4, QO, ROWS), F32),
        ((2, 8, 256, 128), BF),
        ((2, 8, 256, 128), BF),
        ((2, 8, 256, 128), F32),
        ((2, 2, 4, 256, 128), BF),
        ((2, 2, 4, 256, 128), BF),
        ((2, 2, ROWS, 128), BF),
        ((2, 2, ROWS, 128), BF),
    ]
    count = 240
    parts = pl.pallas_call(
        kernel,
        name="critic_layer",
        out_shape=[jax.ShapeDtypeStruct(s, d) for s, d in shapes],
        in_specs=[hbm] * 7,
        out_specs=[vm] * 6,
        scratch_shapes=[pltpu.VMEM(s, d) for s, d in scratch]
        + [pltpu.SemaphoreType.DMA((n,)) for n in (count, count, 7)],
        compiler_params=pltpu.CompilerParams(
            collective_id=0, has_side_effects=True, vmem_limit_bytes=48 << 20),
    )(*(pltpu.with_memory_space_constraint(v, pltpu.HBM)
        for v in (x_store, attn_store, replay_idx, w_qkv, w_out, d_qkv.T, d_out)))
    qkv, *rest = pl.pallas_call(
        spread,
        name="spread",
        out_shape=[jax.ShapeDtypeStruct(s, d) for s, d in shapes],
        in_specs=[hbm] * 6,
        out_specs=[hbm] * 6,
        scratch_shapes=[pltpu.SemaphoreType.DMA((6,))],
        compiler_params=pltpu.CompilerParams(vmem_limit_bytes=1 << 20),
    )(*parts)
    return (qkv.T, *rest)


def solution(mesh):
    in_specs = (
        P("replay", "tensor"),
        P("replay", "tensor"),
        P("replay", None),
        P("tensor", "replay"),
        P("tensor", "replay"),
        P("replay", "tensor"),
        P("replay", "tensor"),
    )
    out_specs = (
        P("replay", "tensor"),
        P("replay", "tensor"),
        P("replay", "tensor"),
        P("replay", "tensor"),
        P("tensor", None),
        P("tensor", None),
    )
    return jax.shard_map(shards, mesh=mesh, in_specs=in_specs, out_specs=out_specs, check_vma=False)
```

```python
import jax
import jax.numpy as jnp
from jax import lax
from jax.experimental import pallas as pl
from jax.experimental.pallas import tpu as pltpu
from jax.sharding import PartitionSpec as P

BF, F32 = jnp.bfloat16, jnp.float32
MESH = pl.DeviceIdType.MESH
ROWS, QF, OF, QO = 128, 192, 128, 320
PARTS = ((0, QF), (QF, OF))
PIECES = ((0, 96), (96, 96), (192, 64), (256, 64))


def dot(a, b, ca, cb):
    return lax.dot_general(a, b, (((ca,), (cb,)), ((), ())), preferred_element_type=F32)


def make_labels():
    table = {}

    def label(*key):
        return table.setdefault(key, len(table))

    return table, label


TABLE, LABEL = make_labels()


def kernel(x_ref, a_ref, idx_ref, wq_ref, wo_ref, dq_ref, do_ref,
           qkv_ref, out_ref, gin_ref, gat_ref, gwq_ref, gwo_ref,
           xin, ain, idx, own, dh, wall, xb, gsend, gkeep, gr, gout,
           ysend, yrecv, ykeep, esend, erecv, part, zsend, zrecv, scsend, screcv,
           ssem, rsem, lsem):
    t, r = lax.axis_index("tensor"), lax.axis_index("replay")
    c, yh, z = lax.rem(t, 2), lax.rem(t // 2, 2), t // 4
    x, yl = r // 4, lax.rem(r, 4)
    h = lax.rem(z, 2)

    def device(x_, yl_, yh_, z_, c_):
        return ((z_ * 2 + yh_) * 2 + c_, x_ * 4 + yl_)

    def xat(k):
        return lax.rem(x + k + 4, 4)

    def yat(k):
        return lax.rem(yl + k + 4, 4)

    def zat(k):
        return lax.rem(z + k + 8, 8)

    xdev = {k: device(xat(k), yl, yh, z, c) for k in (1, -1, 2)}
    zdev = {k: device(x, yl, yh, zat(k), c) for k in (1, -1)}
    ydev = {k: device(x, yat(k), yh, z, c) for k in (1, 2, 3)}
    sib = device(x, yl, yh, z, 1 - c)
    q = 2 * h + yh
    zt = 2 * (z // 2) + yl // 2
    alone = yl == q
    yhs = (yh, 1 - yh)
    to_dev = [device(x, q, v, zt, c) for v in yhs]
    from_dev = [device(x, 2 * h + v, lax.rem(yl, 2), zt, c) for v in yhs]

    loads = [
        pltpu.make_async_copy(src, dst, lsem.at[i])
        for i, (src, dst) in enumerate((
            (idx_ref, idx), (x_ref, xin), (do_ref, own.at[1]),
            (wq_ref, wall.at[x, pl.ds(0, QF)]), (wo_ref, wall.at[x, pl.ds(QF, OF)]),
            (dq_ref, dh.at[yl, pl.ds(0, QF)]), (a_ref, ain)))
    ]
    for cp in loads:
        cp.start()

    bar = pltpu.get_barrier_semaphore()
    peers = list(xdev.values()) + list(zdev.values()) + list(ydev.values()) + [sib]
    for d in peers + to_dev + from_dev:
        pl.semaphore_signal(bar, inc=1, device_id=d, device_id_type=MESH)

    sent = []
    near = jnp.where(yl == 0, 3, 1)
    slot_y = (yl, yat(2), yat(-near), yat(near))
    inner = jnp.logical_and(yl > 0, yl < 3)
    end = 3 * (yl // 2)
    ends = []

    def desc(src, dst, s, rs, dev):
        return pltpu.make_async_remote_copy(
            src_ref=src, dst_ref=dst, send_sem=ssem.at[s], recv_sem=rsem.at[rs],
            device_id=dev, device_id_type=MESH)

    def send(src, dst, dev, *key):
        s = LABEL(*key)
        cp = desc(src, dst, s, s, dev)
        cp.start()
        sent.append(cp)

    def arrive(dst, *key):
        s = LABEL(*key)
        desc(dst, dst, s, s, sib).wait_recv()

    iota0 = lax.broadcasted_iota(jnp.int32, (ROWS, ROWS), 0)
    loads[0].wait()
    loads[1].wait()
    pick = jnp.where(iota0 == idx[...], 1.0, 0.0).astype(BF)
    own[0] = dot(pick, xin[...], 0, 0).astype(BF)
    pl.semaphore_wait(bar, len(peers) + 4)

    def line(block, *key):
        first = LABEL(*key, 1)
        assert (LABEL(*key, 2), LABEL(*key, 3)) == (first + 1, first + 2)

        def go(k, slot):
            s = LABEL(*key, "k", k)
            return desc(block(yl), block(yl), s, first + slot - 1, ydev[k])

        go(2, 1).start()
        pl.when(yl != 3)(lambda: go(1, 2).start())
        pl.when(yl != 0)(lambda: go(3, jnp.where(yl == 1, 2, 3)).start())
        ends.append(lambda: go(2, 1).wait_send())
        ends.append(lambda: pl.when(yl != 3)(lambda: go(1, 2).wait_send()))
        ends.append(lambda: pl.when(yl != 0)(lambda: go(3, 3).wait_send()))

    def line_take(block, slot, *key):
        arrive(block(slot_y[slot]), *key, slot)
        if slot == 1:
            s = LABEL(*key, "k", 0)

            def go():
                return desc(block(yat(2)), block(yat(2)), s, LABEL(*key, 3), device(x, end, yh, z, c))

            pl.when(inner)(lambda: go().start())
            ends.append(lambda: pl.when(inner)(lambda: go().wait_send()))

    def turn(arr):
        dst = xb.at[arr, c, zt, pl.ds(pl.multiple_of(lax.rem(yl, 2) * ROWS, ROWS), ROWS)]
        rs = LABEL("turn", arr, 0) + lax.rem(yl, 2)
        assert LABEL("turn", arr, 1) == LABEL("turn", arr, 0) + 1

        @pl.when(alone)
        def _():
            pltpu.make_async_copy(own.at[arr], dst, rsem.at[rs]).start()

        @pl.when(jnp.logical_not(alone))
        def _():
            desc(own.at[arr], dst, LABEL("turn", arr, 0), rs, to_dev[0]).start()

        desc(own.at[arr], dst, LABEL("turn", arr, 1), rs, to_dev[1]).start()

    def turn_sent(arr):
        @pl.when(jnp.logical_not(alone))
        def _():
            desc(own.at[arr], own.at[arr], LABEL("turn", arr, 0), 0, to_dev[0]).wait_send()

        desc(own.at[arr], own.at[arr], LABEL("turn", arr, 1), 0, to_dev[1]).wait_send()

    turn(0)
    for cp in loads[2:]:
        cp.wait()
    turn(1)
    dh[yl, QF:QO] = dot(ain[...], pick, 0, 0).astype(BF)
    for k in (1, -1, 2):
        send(wall.at[x], wall.at[x], xdev[k], "w", k)

    def zways(step, arr):
        return [w for w in (1, -1) if step < 4 or (arr == 0) == (w == 1)]

    def zblock(core, step, arr, way, v):
        if v is None:
            return xb.at[arr, core, zat(-way * step)]
        return xb.at[arr, core, zat(-way * step), pl.ds(v * ROWS, ROWS)]

    def zpass(step, arr, way, v):
        if way in zways(step, arr):
            piece = zblock(c, step - 1, arr, way, v)
            send(piece, piece, zdev[way], "z", step, arr, way, v)

    def zgive(step, arr, way, v):
        piece = zblock(c, step, arr, way, v)
        send(piece, piece, sib, "s", step, arr, way, v)

    def zfirst(arr):
        for v in (0, 1):
            arrive(zblock(c, 0, arr, 1, v), "turn", arr, v)
        for way in (1, -1):
            zpass(1, arr, way, None)
        zgive(0, arr, 1, None)

    def zstep(step, arr):
        for way in zways(step, arr):
            arrive(zblock(c, step, arr, way, None), "z", step, arr, way, None)
            if step < 4:
                zpass(step + 1, arr, way, None)
        for way in zways(step, arr):
            zgive(step, arr, way, None)

    def other(arr):
        arrive(zblock(1 - c, 0, arr, 1, None), "s", 0, arr, 1, None)
        for step in (1, 2, 3, 4):
            for way in zways(step, arr):
                arrive(zblock(1 - c, step, arr, way, None), "s", step, arr, way, None)

    def block(arr, xp):
        return jnp.concatenate(
            [jnp.concatenate([xb[arr, 0, 2 * xp + v], xb[arr, 1, 2 * xp + v]], axis=1) for v in (0, 1)], axis=0)

    def grads(p):
        lo, n = PARTS[p]
        lhs = jnp.concatenate([dh[g, lo:lo + n] for g in range(4)], axis=1)

        def term(k):
            return dot(lhs, block(p, xat(k)), 1, 0) * (1.0 / ROWS)

        for i, k in enumerate((2, 1, -1)):
            gsend[i, lo:lo + n] = term(k).astype(BF)
            send(gsend.at[i, pl.ds(lo, n)], gr.at[i, pl.ds(lo, n)], xdev[k], "g", p, k)
        gkeep[lo:lo + n] = term(0)

    def grads2(p):
        lo, n = PARTS[p]
        total = gkeep[lo:lo + n]
        for i, k in enumerate((2, 1, -1)):
            arrive(gr.at[i, pl.ds(lo, n)], "g", p, k)
            total = total + gr[i, lo:lo + n].astype(F32)
        gout[r, lo:lo + n] = total.astype(BF)
        for piece in (2 * p, 2 * p + 1):
            lo, n = PIECES[piece]
            mine = gout.at[r, pl.ds(lo, n)]
            line(lambda y: gout.at[x * 4 + y, pl.ds(lo, n)], "ay", piece)
            for k in (1, -1):
                send(mine, mine, xdev[k], "ax", piece, 0, k)

    def gather_y(p, *slots):
        lo, n = PIECES[p]
        for slot in slots:
            line_take(lambda y: gout.at[x * 4 + y, pl.ds(lo, n)], slot, "ay", p)
            piece = gout.at[x * 4 + slot_y[slot], pl.ds(lo, n)]
            for k in (1, -1):
                send(piece, piece, xdev[k], "ax", p, slot, k)

    def gather_x(p, *slots):
        lo, n = PIECES[p]
        half = n // 2
        for slot in slots:
            for k, at in ((1, lo), (-1, lo + half)):
                row = xat(-k) * 4 + slot_y[slot]
                arrive(gout.at[row, pl.ds(lo, n)], "ax", p, slot, k)
                piece = gout.at[row, pl.ds(at, half)]
                send(piece, piece, xdev[k], "ar", p, slot, k)

    def put(k):
        for y in range(4):
            row = xat(k) * 4 + y
            cols = pl.ds(pl.multiple_of(row * 256, 256), 256)
            gwq_ref[:, cols] = gout[row, 0:QF]
            gwo_ref[:, cols] = gout[row, QF:QO]

    def gather_end(p):
        lo, n = PIECES[p]
        half = n // 2
        for slot in range(4):
            for k, at in ((1, lo), (-1, lo + half)):
                arrive(gout.at[xat(2) * 4 + slot_y[slot], pl.ds(at, half)], "ar", p, slot, k)

    def eterm(arr):
        lo, n = PARTS[arr]
        w = jnp.concatenate([wall[v, lo:lo + n] for v in range(4)], axis=1)
        for g in range(4):
            y = dot(dh[g, lo:lo + n], w, 0, 0)
            rows = slice(g % 2 * ROWS, g % 2 * ROWS + ROWS)
            for xp in range(4):
                left, right = y[:, xp * 256:xp * 256 + 128], y[:, xp * 256 + 128:xp * 256 + 256]
                part[arr, 2 * xp + g // 2, rows] = jnp.where(c == 0, left, right)
                esend[arr, 2 * xp + g // 2, rows] = jnp.where(c == 0, right, left).astype(BF)
        send(esend.at[arr], erecv.at[arr], sib, "e", arr)

    def yterm(arr):
        lo, n = PARTS[arr]
        w = jnp.concatenate([wall[v, lo:lo + n] for v in range(4)], axis=1)
        for v in (0, 1):
            rhs = jnp.concatenate([xb[arr, cc, 2 * xp + v] for xp in range(4) for cc in (0, 1)], axis=1)
            y = dot(w, rhs, 1, 1)
            for j in (0, 1):
                ykeep[2 * v + j, lo:lo + n] = y[:, j * ROWS:(j + 1) * ROWS]
                ysend[2 * v + j, lo:lo + n] = y[:, j * ROWS:(j + 1) * ROWS].astype(BF)

    def ygo(arr):
        lo, n = PARTS[arr]
        for k in (1, 2, 3):
            send(ysend.at[yat(k), pl.ds(lo, n)], yrecv.at[k - 1, pl.ds(lo, n)], ydev[k], "y", arr, k)

    def zadd(step):
        for arr in (0, 1):
            if step == 1:
                arrive(erecv.at[arr], "e", arr)
                for v in range(8):
                    part[arr, v] = part[arr, v] + erecv[arr, v].astype(F32)
            for way in (1, -1):
                i = (1 - way) // 2
                if step == 1 and (arr == 0) != (way == 1):
                    continue
                at = zat(way * (5 - step))
                value = part[arr, at]
                if step > 2 or (step == 2 and (arr == 0) == (way == 1)):
                    arrive(zrecv.at[arr, i, step - 2], "r", step - 1, arr, way)
                    value = value + zrecv[arr, i, step - 2].astype(F32)
                zsend[arr, i, step - 1] = value.astype(BF)
                send(zsend.at[arr, i, step - 1], zrecv.at[arr, i, step - 1], zdev[way], "r", step, arr, way)

    def zend():
        for arr in (0, 1):
            value = part[arr, z]
            for way in (1, -1):
                i = (1 - way) // 2
                arrive(zrecv.at[arr, i, 3], "r", 4, arr, way)
                value = value + zrecv[arr, i, 3].astype(F32)
            value = value.astype(BF)
            for j in (0, 1):
                scsend[j, arr] = value[j * ROWS:(j + 1) * ROWS]

    def scatter():
        rs = LABEL("sc", 0) + yh
        assert LABEL("sc", 1) == LABEL("sc", 0) + 1
        dst = screcv.at[yh]

        @pl.when(alone)
        def _():
            pltpu.make_async_copy(scsend.at[yhs[0]], dst, rsem.at[rs]).start()

        @pl.when(jnp.logical_not(alone))
        def _():
            desc(scsend.at[yhs[0]], dst, LABEL("sc", 0), rs, from_dev[0]).start()

        desc(scsend.at[yhs[1]], dst, LABEL("sc", 1), rs, from_dev[1]).start()

    def scatter_end():
        for v in (0, 1):
            arrive(screcv.at[v], "sc", v)
        gin_ref[...] = screcv[0, 0].astype(F32) + screcv[1, 0].astype(F32)
        out_ref[...] = screcv[0, 1].astype(F32) + screcv[1, 1].astype(F32)

        @pl.when(jnp.logical_not(alone))
        def _():
            desc(scsend.at[0], scsend.at[0], LABEL("sc", 0), 0, from_dev[0]).wait_send()

        desc(scsend.at[0], scsend.at[0], LABEL("sc", 1), 0, from_dev[1]).wait_send()

    def dhblock(y):
        return dh.at[y]

    zfirst(0)
    line(dhblock, "dh")

    zfirst(1)

    for arr in (0, 1):
        zstep(1, arr)

    for arr in (0, 1):
        zstep(2, arr)

    line_take(dhblock, 1, "dh")
    for arr in (0, 1):
        zstep(3, arr)

    line_take(dhblock, 2, "dh")
    line_take(dhblock, 3, "dh")

    for k in (1, -1, 2):
        arrive(wall.at[xat(-k)], "w", k)
    eterm(0)
    zstep(4, 0)
    other(0)

    grads(0)

    eterm(1)
    yterm(0)
    ygo(0)

    zstep(4, 1)
    other(1)
    grads(1)
    yterm(1)
    ygo(1)

    zadd(1)

    grads2(0)

    zadd(2)

    grads2(1)

    gather_x(0, 0)
    gather_y(0, 1, 2, 3)

    zadd(3)
    gather_x(1, 0)
    gather_y(1, 1, 2, 3)

    gather_x(0, 1, 2, 3)
    zadd(4)
    gather_x(2, 0)
    gather_y(2, 1, 2, 3)

    zend()
    scatter()

    gather_x(1, 1, 2, 3)
    gather_x(3, 0)
    gather_y(3, 1, 2, 3)

    gather_x(2, 1, 2, 3)

    put(0)
    gather_x(3, 1, 2, 3)
    put(1)
    put(-1)

    total = ykeep[yl]
    for k in (1, 2, 3):
        for arr, (lo, n) in enumerate(PARTS):
            arrive(yrecv.at[k - 1, pl.ds(lo, n)], "y", arr, k)
        total = total + yrecv[k - 1].astype(F32)
    qkv_ref[...] = total[0:QF]
    gat_ref[...] = total[QF:QO].T

    scatter_end()

    for p in range(4):
        gather_end(p)

    put(2)
    turn_sent(0)
    turn_sent(1)
    for cp in sent:
        cp.wait_send()
    for wait in ends:
        wait()


def spread(*refs):
    n = len(refs) // 2
    copies = [pltpu.make_async_copy(refs[i], refs[n + i], refs[2 * n].at[i]) for i in range(n)]
    for cp in copies:
        cp.start()
    for cp in copies:
        cp.wait()


def shards(x_store, attn_store, replay_idx, w_qkv, w_out, d_qkv, d_out):
    vm, hbm = pl.BlockSpec(memory_space=pltpu.VMEM), pl.BlockSpec(memory_space=pl.ANY)
    shapes = [((QF, ROWS), F32), ((ROWS, 128), F32), ((ROWS, 128), F32), ((ROWS, 128), F32),
              ((QF, 4096), BF), ((OF, 4096), BF)]
    scratch = [
        ((ROWS, 128), BF),
        ((ROWS, 128), BF),
        ((1, ROWS), jnp.int32),
        ((2, ROWS, 128), BF),
        ((4, QO, ROWS), BF),
        ((4, QO, 256), BF),
        ((2, 2, 8, 256, 128), BF),
        ((3, QO, 256), BF),
        ((QO, 256), F32),
        ((3, QO, 256), BF),
        ((16, QO, 256), BF),
        ((4, QO, ROWS), BF),
        ((3, QO, ROWS), BF),
        ((4, QO, ROWS), F32),
        ((2, 8, 256, 128), BF),
        ((2, 8, 256, 128), BF),
        ((2, 8, 256, 128), F32),
        ((2, 2, 4, 256, 128), BF),
        ((2, 2, 4, 256, 128), BF),
        ((2, 2, ROWS, 128), BF),
        ((2, 2, ROWS, 128), BF),
    ]
    count = 240
    parts = pl.pallas_call(
        kernel,
        name="critic_layer",
        out_shape=[jax.ShapeDtypeStruct(s, d) for s, d in shapes],
        in_specs=[hbm] * 7,
        out_specs=[vm] * 6,
        scratch_shapes=[pltpu.VMEM(s, d) for s, d in scratch]
        + [pltpu.SemaphoreType.DMA((n,)) for n in (count, count, 7)],
        compiler_params=pltpu.CompilerParams(
            collective_id=0, has_side_effects=True, vmem_limit_bytes=48 << 20),
    )(*(pltpu.with_memory_space_constraint(v, pltpu.HBM)
        for v in (x_store, attn_store, replay_idx, w_qkv, w_out, d_qkv.T, d_out)))
    qkv, *rest = pl.pallas_call(
        spread,
        name="spread",
        out_shape=[jax.ShapeDtypeStruct(s, d) for s, d in shapes],
        in_specs=[hbm] * 6,
        out_specs=[hbm] * 6,
        scratch_shapes=[pltpu.SemaphoreType.DMA((6,))],
        compiler_params=pltpu.CompilerParams(vmem_limit_bytes=1 << 20),
    )(*parts)
    return (qkv.T, *rest)


def solution(mesh):
    in_specs = (
        P("replay", "tensor"),
        P("replay", "tensor"),
        P("replay", None),
        P("tensor", "replay"),
        P("tensor", "replay"),
        P("replay", "tensor"),
        P("replay", "tensor"),
    )
    out_specs = (
        P("replay", "tensor"),
        P("replay", "tensor"),
        P("replay", "tensor"),
        P("replay", "tensor"),
        P("tensor", None),
        P("tensor", None),
    )
    return jax.shard_map(shards, mesh=mesh, in_specs=in_specs, out_specs=out_specs, check_vma=False)
```
